128 devices in a mesh: ctx: 32 (over x, z, core), tp: 4 (over y).
Axes of the slice: x: 4, y: 4, z: 4, core: 2. Of those that a mesh axis runs over, the one named last changes fastest.
Arguments:
- projected: float32 [3, 16384, 4096], P(None, 'ctx', 'tp'), may hold values from -6 to 6
- short_filters: float32 [3, 3, 4096], P(None, None, 'tp'), may hold values from -3 to 3
- long_filter: float32 [16384, 4096], P('ctx', 'tp'), may hold values from -1.1 to 1.1, as said below
- skip_gain: float32 [4096], P('tp'), may hold values from -3 to 3
- out_weight: bfloat16 [4096, 4096], P('tp'), may hold values from -0.09375 to 0.09375
Outputs:
- mixer_out: float32 [16384, 4096], P('ctx', 'tp')
The draws below stay inside these ranges and needn't reach their ends.
Inputs may be any that keep to these rules, and one draw needn't show every extreme that they name: `long_filter`: each channel's filter decays along the tokens; no further structure is promised.
All inputs are finite; a program needn't handle non-finite values.
Results may differ from the reference program's by a relative error of at most 0.0029.
Values sent between devices are 32-bit elements; how exact they have to be, the bound alone decides.
A program may use at most 192 MiB of HBM per device.

```python
import math
import jax
import jax.numpy as jnp
from jax import lax

D = 4096
TOKENS = 16384


def draw_long_filter(key, part):
    key = jax.random.fold_in(key, 11)
    keys = jax.random.split(key, 6)
    slow_tenths = 5
    slow_flags = jax.random.randint(keys[0], (D,), 0, 10) < slow_tenths
    slow_rate = jnp.exp(jax.random.uniform(keys[1], (D,), jnp.float32, math.log(0.2 / TOKENS), math.log(1.5 / TOKENS)))
    fast_rate = jnp.exp(jax.random.uniform(keys[2], (D,), jnp.float32, math.log(1.0 / 50.0), math.log(1.0 / 30.0)))
    rates = jnp.where(slow_flags, slow_rate, fast_rate)
    position_grid = jnp.arange(TOKENS, dtype=jnp.float32)[:, None]
    decay_window = jnp.exp(-rates[None, :] * position_grid)
    sample_locations = jax.random.randint(keys[3], (3, D), 0, TOKENS).astype(jnp.float32)
    decay_factors = jax.random.uniform(keys[4], (3, D), jnp.float32, 0.5, 0.8)
    for impulse_train in range(3):
        decay_window = decay_window * jnp.where(position_grid >= sample_locations[impulse_train][None, :], decay_factors[impulse_train][None, :], 1.0)
    amplitude = jnp.sqrt(2.0 * rates / (1.0 - jnp.exp(-2.0 * rates * TOKENS)))
    noise = jnp.clip(jax.random.normal(keys[5], (TOKENS, D), jnp.float32), -4.0, 4.0)
    return (decay_window * amplitude[None, :] * noise).astype(jnp.float32)


def levels(key, dims, pieces, least, largest):
    level = 1.0
    for axis_at, parts in pieces:
        steps = jax.random.uniform(jax.random.fold_in(jax.random.fold_in(key, 6), axis_at), (parts,), jnp.float32, least / len(pieces), largest / len(pieces))
        level = level * jnp.repeat(jnp.exp(steps), dims[axis_at] // parts).reshape((-1,) + (1,) * (len(dims) - 1 - axis_at))
    return level


def gaussian(stream_key, shape, scale, bound, pieces=(), kind=jnp.bfloat16):
    drawn = scale * jax.random.normal(stream_key, shape, jnp.float32)
    if pieces:
        drawn = drawn * levels(stream_key, shape, pieces, -0.22, 0.18)
    return jnp.clip(drawn, -bound, bound).astype(kind)


def setup_inputs(seed: int = 0) -> dict:
    arg_keys = jax.random.split(jax.random.key(seed), 6)
    return {
        "projected": gaussian(arg_keys[0], (3, TOKENS, D), 1.0, 6.0, ((1, 32), (2, 4)), jnp.float32),
        "short_filters": gaussian(arg_keys[1], (3, 3, D), 0.6, 3.0, ((2, 4),), jnp.float32),
        "long_filter": draw_long_filter(jax.random.fold_in(arg_keys[5], 71), 0),
        "skip_gain": gaussian(arg_keys[3], (D,), 1.0, 3.0, ((0, 4),), jnp.float32),
        "out_weight": gaussian(arg_keys[4], (D, D), D ** -0.5, 0.09375, ((0, 4),)),
    }


def short_conv(streams, short_filters):
    length = streams.shape[1]
    padded = jnp.pad(streams, ((0, 0), (2, 0), (0, 0)))
    tap_zero = short_filters[:, 0][:, None, :] * padded[:, 2:2 + length]
    tap_one = short_filters[:, 1][:, None, :] * padded[:, 1:1 + length]
    tap_two = short_filters[:, 2][:, None, :] * padded[:, 0:length]
    return tap_zero + tap_one + tap_two


def causal_conv(signal, filt):
    length = signal.shape[0]
    spectrum = jnp.fft.rfft(signal, n=2 * length, axis=0) * jnp.fft.rfft(filt, n=2 * length, axis=0)
    return jnp.fft.irfft(spectrum, n=2 * length, axis=0)[:length]


def reference(projected, short_filters, long_filter, skip_gain, out_weight):
    truncated_filter = short_conv(projected, short_filters)
    gated = truncated_filter[1] * truncated_filter[2]
    length, width = gated.shape
    block_width = min(512, width)
    block_count = width // block_width
    signal_blocks = jnp.transpose(gated.reshape(length, block_count, block_width), (1, 0, 2))
    filter_blocks = jnp.transpose(long_filter.reshape(length, block_count, block_width), (1, 0, 2))
    conv_blocks = lax.map(lambda pair: causal_conv(pair[0], pair[1]), (signal_blocks, filter_blocks))
    conv = jnp.transpose(conv_blocks, (1, 0, 2)).reshape(length, width)
    mixed = conv + skip_gain[None, :] * gated
    gated_out = (truncated_filter[0] * mixed).astype(jnp.bfloat16)
    return jnp.dot(gated_out, out_weight, preferred_element_type=jnp.float32)
```

```python
import functools

import jax
import jax.numpy as jnp
import ml_dtypes
import numpy as np
from jax import lax
from jax.experimental import pallas as pl
from jax.experimental.pallas import tpu as pltpu
from jax.sharding import PartitionSpec as P

MESH = pl.DeviceIdType.MESH
BF16 = jnp.bfloat16
F32 = jnp.float32
CTX = 32
TP = 4
OWN = 32
GROUP = 8
CHIP_OFFSETS = (
    (1, 0), (3, 0), (0, 1), (0, 3), (1, 1), (3, 3), (1, 3), (3, 1),
    (2, 0), (0, 2), (2, 1), (2, 3), (1, 2), (3, 2), (2, 2),
)
PEERS = tuple((a, b, d) for a, b in CHIP_OFFSETS for d in (0, 1)) + ((0, 0, 1),)


def split_np(table):
    high = table.astype(ml_dtypes.bfloat16)
    low = (table - high.astype(np.float64)).astype(ml_dtypes.bfloat16)
    return high, low


def tables():
    block = np.arange(32)
    n1 = np.concatenate([2 * block, 2 * block + 1]).astype(np.float64)
    k1 = np.arange(64) + 0.25
    n2 = np.arange(256)
    psi = 2 * np.pi * np.outer(k1, n1) / 64
    high, low = split_np(np.concatenate([np.cos(psi), -np.sin(psi)], 0))
    first = np.concatenate([high, high, low], 1)
    phi = 2 * np.pi * np.outer(k1, n2) / 16384
    twist = np.stack([np.cos(phi), np.sin(phi)]).astype(np.float32)
    theta = 2 * np.pi * (np.outer(n2, n2) % 256) / 256
    cosine, sine = np.cos(theta), np.sin(theta)
    high, low = split_np(np.block([[cosine, -sine], [sine, cosine]]))
    second = np.concatenate([high, high, low], 0)
    high, low = split_np(np.block([[cosine, sine], [-sine, cosine]]))
    back_second = np.concatenate([high, high, low], 0)
    high, low = split_np(np.concatenate([np.cos(psi.T), -np.sin(psi.T)], 1) / 16384)
    back_first = np.concatenate([high, high, low], 1)
    return first, twist, second, back_second, back_first


def split(value):
    high = value.astype(BF16)
    return high, (value - high.astype(F32)).astype(BF16)


def dot(left, right):
    return jnp.dot(left, right, preferred_element_type=F32)


def ctx_peer(me, offset):
    a, b, d = offset
    return (me // 8 + a) % 4 * 8 + (me // 2 + b) % 4 * 2 + (me + d) % 2


def greet_ctx(barrier, me, tp):
    def signal(i, carry):
        pl.semaphore_signal(
            barrier, inc=1, device_id=(lax.rem(me + i, CTX), tp), device_id_type=MESH
        )
        return carry

    lax.fori_loop(1, CTX, signal, 0)


def rows_of(device):
    return pl.ds(pl.multiple_of(device * OWN, OWN), OWN)


def send_all(source, target, me, tp, send_sem, recv_sem, pieces):
    pltpu.make_async_copy(
        source.at[:, rows_of(me), :], target.at[:, rows_of(me), :], recv_sem
    ).start()
    step = source.shape[0] // pieces
    for piece in range(pieces):
        for offset in PEERS:
            peer = ctx_peer(me, offset)
            part = pl.ds(piece * step, step)
            pltpu.make_async_remote_copy(
                src_ref=source.at[part, rows_of(peer), :],
                dst_ref=target.at[part, rows_of(me), :],
                send_sem=send_sem,
                recv_sem=recv_sem,
                device_id=(peer, tp),
                device_id_type=MESH,
            ).start()


def wait_arrived(target, recv_sem):
    pltpu.make_async_copy(target, target, recv_sem).wait()


def wait_sent(source, send_sem):
    away = source.at[:, 0 : (CTX - 1) * OWN, :]
    pltpu.make_async_copy(away, away, send_sem).wait()


def short_conv(projected, halo, short_filters, stream, jb, cols):
    rows = projected[stream, jb * 128 : jb * 128 + 128, cols]
    before = halo[stream, :, cols] if jb == 0 else projected[stream, jb * 128 - 8 : jb * 128, cols]
    longer = jnp.concatenate([before, rows], 0)
    taps = short_filters[stream, :, cols]
    return taps[0:1] * rows + taps[1:2] * longer[7:135] + taps[2:3] * longer[6:134]


def spread_kernel(
    projected, short_filters, long_filter, filt, signal, gated, shortened_q,
    halo, halo_in, filt_t, gated_t, send_sem, recv_sem, halo_send, halo_recv,
):
    me = lax.axis_index("ctx")
    tp = lax.axis_index("tp")
    barrier = pltpu.get_barrier_semaphore()
    greet_ctx(barrier, me, tp)

    def turn_filter(cb, carry):
        cols = pl.ds(pl.multiple_of(cb * 128, 128), 128)
        for jb in range(4):
            filt_t[jb, cols, :] = long_filter[jb * 128 : jb * 128 + 128, cols].T
        return carry

    lax.fori_loop(0, 8, turn_filter, 0)
    pl.semaphore_wait(barrier, CTX - 1)
    edge = pltpu.make_async_remote_copy(
        src_ref=projected.at[:, 504:512, :],
        dst_ref=halo_in,
        send_sem=halo_send,
        recv_sem=halo_recv,
        device_id=(lax.rem(me + 1, CTX), tp),
        device_id_type=MESH,
    )
    edge.start()
    send_all(filt_t, filt, me, tp, send_sem.at[0], recv_sem.at[0], 2)
    edge.wait()
    halo[...] = jnp.where(me > 0, halo_in[...], 0.0)

    def gate(cb, carry):
        cols = pl.ds(pl.multiple_of(cb * 128, 128), 128)
        for jb in range(4):
            key = short_conv(projected, halo, short_filters, 1, jb, cols)
            value = short_conv(projected, halo, short_filters, 2, jb, cols)
            product = key * value
            gated[jb * 128 : jb * 128 + 128, cols] = product
            gated_t[jb, cols, :] = product.T
        return carry

    lax.fori_loop(0, 8, gate, 0)
    send_all(gated_t, signal, me, tp, send_sem.at[1], recv_sem.at[1], 2)

    def query(cb, carry):
        cols = pl.ds(pl.multiple_of(cb * 128, 128), 128)
        for jb in range(4):
            shortened_q[jb * 128 : jb * 128 + 128, cols] = short_conv(
                projected, halo, short_filters, 0, jb, cols
            )
        return carry

    lax.fori_loop(0, 8, query, 0)
    wait_sent(filt_t, send_sem.at[0])
    wait_sent(gated_t, send_sem.at[1])
    wait_arrived(filt, recv_sem.at[0])
    wait_arrived(signal, recv_sem.at[1])


def conv_kernel(
    filt, signal, first, twist, second, back_second, back_first, out, rows, spectrum, inner
):
    cosine, sine = twist[0], twist[1]

    def forward(source, group):
        for i in range(GROUP):
            one = pl.ds(group * GROUP + i, CTX, stride=OWN)
            blocks = [source[jb, one, :] for jb in range(4)]
            high, low = split(
                jnp.concatenate(
                    [jnp.concatenate(blocks[:2], 1), jnp.concatenate(blocks[2:], 1)], 0
                )
            )
            turned = dot(first[...], jnp.concatenate([high, low, high], 0))
            real, imag = turned[:64], turned[64:]
            real_high, real_low = split(real * cosine + imag * sine)
            imag_high, imag_low = split(imag * cosine - real * sine)
            rows[i * 64 : i * 64 + 64, :] = jnp.concatenate(
                [real_high, imag_high, real_low, imag_low, real_high, imag_high], 1
            )
        return dot(rows[...], second[...])

    def group_rows(group):
        return pl.ds(pl.multiple_of(group * GROUP * 64, GROUP * 64), GROUP * 64)

    def filter_step(group, carry):
        spectrum[group_rows(group), :] = forward(filt, group)
        return carry

    lax.fori_loop(0, OWN // GROUP, filter_step, 0)

    def signal_step(group, carry):
        left = forward(signal, group)
        right = spectrum[group_rows(group), :]
        left_real, left_imag = left[:, :256], left[:, 256:]
        right_real, right_imag = right[:, :256], right[:, 256:]
        real_high, real_low = split(left_real * right_real - left_imag * right_imag)
        imag_high, imag_low = split(left_real * right_imag + left_imag * right_real)
        product = jnp.concatenate(
            [real_high, imag_high, real_low, imag_low, real_high, imag_high], 1
        )
        inner[group_rows(group), :] = dot(product, back_second[...])
        return carry

    lax.fori_loop(0, OWN // GROUP, signal_step, 0)

    def back_step(group, carry):
        for i in range(GROUP):
            channel = group * GROUP + i
            both = inner[pl.ds(pl.multiple_of(channel * 64, 64), 64), :]
            real, imag = both[:, :256], both[:, 256:]
            real_high, real_low = split(real * cosine - imag * sine)
            imag_high, imag_low = split(imag * cosine + real * sine)
            result = dot(
                back_first[...],
                jnp.concatenate(
                    [real_high, imag_high, real_low, imag_low, real_high, imag_high], 0
                ),
            )
            for jb in range(4):
                out[jb, pl.ds(channel, CTX, stride=OWN), :] = result[
                    jb // 2 * 32 : jb // 2 * 32 + 32, jb % 2 * 128 : jb % 2 * 128 + 128
                ]
        return carry

    lax.fori_loop(0, OWN // GROUP, back_step, 0)


def project_kernel(
    conv, gated, shortened_q, skip_gain, weight_hbm, out,
    weight, conv_in, gated_out, far, near, far_in, near_in,
    send_sem, recv_sem, far_send, far_recv, near_send, near_recv, weight_sem,
):
    me = lax.axis_index("ctx")
    tp = lax.axis_index("tp")
    barrier = pltpu.get_barrier_semaphore()
    greet_ctx(barrier, me, tp)
    up, down = lax.rem(tp + 1, TP), lax.rem(tp + TP - 1, TP)
    for side in (up, down):
        pl.semaphore_signal(barrier, inc=1, device_id=(me, side), device_id_type=MESH)
    load = pltpu.make_async_copy(weight_hbm, weight, weight_sem)
    load.start()
    pl.semaphore_wait(barrier, CTX + 1)
    for jb in range(4):
        chunk = pl.ds(jb, 1)
        send_all(conv.at[chunk], conv_in.at[chunk], me, tp, send_sem.at[jb], recv_sem.at[jb], 1)
    load.wait()

    def columns(quarter):
        return pl.ds(pl.multiple_of(quarter * 1024, 1024), 1024)

    def to_far(jb, side):
        half = slice(512 * side, 512 * side + 512)
        return pltpu.make_async_remote_copy(
            src_ref=far.at[jb, :, half],
            dst_ref=far_in.at[jb, :, half],
            send_sem=far_send.at[jb, side],
            recv_sem=far_recv.at[jb, side],
            device_id=(me, (up, down)[side]),
            device_id_type=MESH,
        )

    def to_near(jb, side):
        return pltpu.make_async_remote_copy(
            src_ref=near.at[jb, side],
            dst_ref=near_in.at[jb, side],
            send_sem=near_send.at[jb, side],
            recv_sem=near_recv.at[jb, side],
            device_id=(me, (up, down)[side]),
            device_id_type=MESH,
        )

    def compute(jb):
        wait_arrived(conv_in.at[pl.ds(jb, 1)], recv_sem.at[jb])
        tokens = slice(jb * 128, jb * 128 + 128)
        mixed = conv_in[jb].T + skip_gain[...] * gated[tokens, :]
        gated_out[...] = (shortened_q[tokens, :] * mixed).astype(BF16)
        far[jb] = dot(gated_out[...], weight[:, columns(lax.rem(tp + 2, TP))])
        to_far(jb, 0).start()
        to_far(jb, 1).start()
        near[jb, 0] = dot(gated_out[...], weight[:, columns(up)])
        near[jb, 1] = dot(gated_out[...], weight[:, columns(down)])
        out[tokens, :] = dot(gated_out[...], weight[:, columns(tp)])

    def relay(jb):
        for side in (0, 1):
            half = slice(512 * side, 512 * side + 512)
            to_far(jb, side).wait_recv()
            near[jb, side, :, half] += far_in[jb, :, half]
            to_near(jb, side).start()

    compute(0)
    for jb in range(1, 4):
        compute(jb)
        relay(jb - 1)
    relay(3)
    for jb in range(4):
        tokens = slice(jb * 128, jb * 128 + 128)
        to_near(jb, 0).wait_recv()
        to_near(jb, 1).wait_recv()
        out[tokens, :] += near_in[jb, 0] + near_in[jb, 1]
    for jb in range(4):
        wait_sent(conv.at[pl.ds(jb, 1)], send_sem.at[jb])
        for side in (0, 1):
            to_far(jb, side).wait_send()
            to_near(jb, side).wait_send()


VMEM = pl.BlockSpec(memory_space=pltpu.VMEM)
ANY = pl.BlockSpec(memory_space=pl.ANY)
DMA = pltpu.SemaphoreType.DMA


def array(*shape):
    return jax.ShapeDtypeStruct(shape, F32)


def per_device(projected, short_filters, long_filter, skip_gain, out_weight):
    filt, signal, gated, shortened_q = pl.pallas_call(
        spread_kernel,
        out_shape=(array(4, 1024, 128), array(4, 1024, 128), array(512, 1024), array(512, 1024)),
        in_specs=[VMEM] * 3,
        out_specs=(VMEM,) * 4,
        scratch_shapes=[
            pltpu.VMEM((3, 8, 1024), F32),
            pltpu.VMEM((3, 8, 1024), F32),
            pltpu.VMEM((4, 1024, 128), F32),
            pltpu.VMEM((4, 1024, 128), F32),
            DMA((2,)),
            DMA((2,)),
            DMA,
            DMA,
        ],
        compiler_params=pltpu.CompilerParams(
            collective_id=0, has_side_effects=True, vmem_limit_bytes=48 * 2**20
        ),
        name="spread",
    )(projected, short_filters, long_filter)
    conv = pl.pallas_call(
        conv_kernel,
        out_shape=array(4, 1024, 128),
        in_specs=[VMEM] * 7,
        out_specs=VMEM,
        scratch_shapes=[
            pltpu.VMEM((GROUP * 64, 1536), BF16),
            pltpu.VMEM((OWN * 64, 512), F32),
            pltpu.VMEM((OWN * 64, 512), F32),
        ],
        compiler_params=pltpu.CompilerParams(vmem_limit_bytes=48 * 2**20),
        name="conv",
    )(filt, signal, *[jnp.asarray(table) for table in tables()])
    return pl.pallas_call(
        project_kernel,
        out_shape=array(512, 1024),
        in_specs=[VMEM] * 4 + [ANY],
        out_specs=VMEM,
        scratch_shapes=[
            pltpu.VMEM((1024, 4096), BF16),
            pltpu.VMEM((4, 1024, 128), F32),
            pltpu.VMEM((128, 1024), BF16),
            pltpu.VMEM((4, 128, 1024), F32),
            pltpu.VMEM((4, 2, 128, 1024), F32),
            pltpu.VMEM((4, 128, 1024), F32),
            pltpu.VMEM((4, 2, 128, 1024), F32),
            DMA((4,)),
            DMA((4,)),
            DMA((4, 2)),
            DMA((4, 2)),
            DMA((4, 2)),
            DMA((4, 2)),
            DMA,
        ],
        compiler_params=pltpu.CompilerParams(
            collective_id=1, has_side_effects=True, vmem_limit_bytes=48 * 2**20
        ),
        name="project",
    )(conv, gated, shortened_q, skip_gain[None], out_weight)


def solution(mesh):
    return jax.shard_map(
        per_device,
        mesh=mesh,
        in_specs=(
            P(None, "ctx", "tp"),
            P(None, None, "tp"),
            P("ctx", "tp"),
            P("tp"),
            P("tp", None),
        ),
        out_specs=P("ctx", "tp"),
        check_vma=False,
    )
```

```python
import jax
import jax.numpy as jnp
import ml_dtypes
import numpy as np
from jax import lax
from jax.experimental import pallas as pl
from jax.experimental.pallas import tpu as pltpu
from jax.sharding import PartitionSpec as P

MESH = pl.DeviceIdType.MESH
BF16 = jnp.bfloat16
F32 = jnp.float32
CTX = 32
TP = 4
OWN = 32
GROUP = 8
GROUPS = OWN // GROUP
CHIP_OFFSETS = (
    (1, 0), (3, 0), (0, 1), (0, 3), (1, 1), (3, 3), (1, 3), (3, 1),
    (2, 0), (0, 2), (2, 1), (2, 3), (1, 2), (3, 2), (2, 2),
)
PEERS = tuple((a, b, d) for a, b in CHIP_OFFSETS for d in (0, 1)) + ((0, 0, 1),)


def split_np(table):
    high = table.astype(ml_dtypes.bfloat16)
    low = (table - high.astype(np.float64)).astype(ml_dtypes.bfloat16)
    return high, low


def tables():
    block = np.arange(32)
    n1 = np.concatenate([2 * block, 2 * block + 1]).astype(np.float64)
    k1 = np.arange(64) + 0.25
    n2 = np.arange(256)
    psi = 2 * np.pi * np.outer(k1, n1) / 64
    high, low = split_np(np.concatenate([np.cos(psi), -np.sin(psi)], 0))
    first = np.concatenate([high, high, low], 1)
    phi = 2 * np.pi * np.outer(k1, n2) / 16384
    twist = np.stack([np.cos(phi), np.sin(phi)]).astype(np.float32)
    theta = 2 * np.pi * (np.outer(n2, n2) % 256) / 256
    cosine, sine = np.cos(theta), np.sin(theta)
    high, low = split_np(np.block([[cosine, -sine], [sine, cosine]]))
    second = np.concatenate([high, high, low], 0)
    high, low = split_np(np.block([[cosine, sine], [-sine, cosine]]))
    back_second = np.concatenate([high, high, low], 0)
    high, low = split_np(np.concatenate([np.cos(psi.T), -np.sin(psi.T)], 1) / 16384)
    back_first = np.concatenate([high, high, low], 1)
    return first, twist, second, back_second, back_first


def split(value):
    high = value.astype(BF16)
    return high, (value - high.astype(F32)).astype(BF16)


def dot(left, right):
    return jnp.dot(left, right, preferred_element_type=F32)


def ctx_peer(me, offset):
    a, b, d = offset
    return (me // 8 + a) % 4 * 8 + (me // 2 + b) % 4 * 2 + (me + d) % 2


def rows_of(device):
    return pl.ds(pl.multiple_of(device * OWN, OWN), OWN)


def send_slabs(source, target, slab, own_slab, me, tp, send_sem, recv_sem):
    pltpu.make_async_copy(
        source.at[:, slab(me), :], target.at[:, own_slab, :], recv_sem
    ).start()
    for offset in PEERS:
        peer = ctx_peer(me, offset)
        pltpu.make_async_remote_copy(
            src_ref=source.at[:, slab(peer), :],
            dst_ref=target.at[:, own_slab, :],
            send_sem=send_sem,
            recv_sem=recv_sem,
            device_id=(peer, tp),
            device_id_type=MESH,
        ).start()


def wait_arrived(target, recv_sem):
    pltpu.make_async_copy(target, target, recv_sem).wait()


def wait_sent(source, send_sem):
    away = source.at[:, 0 : (CTX - 1) * OWN, :]
    pltpu.make_async_copy(away, away, send_sem).wait()


def short_conv(projected, halo, short_filters, stream, jb, cols):
    rows = projected[stream, jb * 128 : jb * 128 + 128, cols]
    before = halo[stream, :, cols] if jb == 0 else projected[stream, jb * 128 - 8 : jb * 128, cols]
    longer = jnp.concatenate([before, rows], 0)
    taps = short_filters[stream, :, cols]
    return taps[0:1] * rows + taps[1:2] * longer[7:135] + taps[2:3] * longer[6:134]


def mixer_kernel(
    projected_hbm, short_filters, long_filter_hbm, skip_gain, weight_hbm,
    first, twist, second, back_second, back_first,
    out,
    projected, long_filter, weight, halo, halo_in, filt_t, gated_t, filt, signal,
    gated, shortened_q, rows, spectrum, conv_in, gated_out, far, near, far_in, near_in,
    load_sem, halo_send, halo_recv, filt_send, filt_recv, signal_send, signal_recv,
    conv_send, conv_recv, far_send, far_recv, near_send, near_recv,
):
    me = lax.axis_index("ctx")
    tp = lax.axis_index("tp")
    up, down = lax.rem(tp + 1, TP), lax.rem(tp + TP - 1, TP)
    conv = filt_t

    barrier = pltpu.get_barrier_semaphore()

    def signal_peer(i, carry):
        pl.semaphore_signal(
            barrier, inc=1, device_id=(lax.rem(me + i, CTX), tp), device_id_type=MESH
        )
        return carry

    lax.fori_loop(1, CTX, signal_peer, 0)
    for side in (up, down):
        pl.semaphore_signal(barrier, inc=1, device_id=(me, side), device_id_type=MESH)
    load_filter = pltpu.make_async_copy(long_filter_hbm, long_filter, load_sem.at[0])
    load_filter.start()
    load_projected = pltpu.make_async_copy(projected_hbm, projected, load_sem.at[1])
    load_projected.start()
    load_weight = pltpu.make_async_copy(weight_hbm, weight, load_sem.at[2])
    load_weight.start()
    load_filter.wait()

    def turn_filter(cb, carry):
        cols = pl.ds(pl.multiple_of(cb * 128, 128), 128)
        for jb in range(4):
            filt_t[jb, cols, :] = long_filter[jb * 128 : jb * 128 + 128, cols].T
        return carry

    lax.fori_loop(0, 8, turn_filter, 0)
    pl.semaphore_wait(barrier, CTX + 1)

    edge = pltpu.make_async_remote_copy(
        src_ref=projected_hbm.at[:, 504:512, :],
        dst_ref=halo_in,
        send_sem=halo_send,
        recv_sem=halo_recv,
        device_id=(lax.rem(me + 1, CTX), tp),
        device_id_type=MESH,
    )
    edge.start()
    for half in range(2):
        part = pl.ds(2 * half, 2)
        send_slabs(
            filt_t.at[part], filt.at[part], rows_of, rows_of(me), me, tp, filt_send, filt_recv
        )
    load_projected.wait()
    edge.wait()
    halo[...] = jnp.where(me > 0, halo_in[...], 0.0)

    def gate(cb, carry):
        cols = pl.ds(pl.multiple_of(cb * 128, 128), 128)
        for jb in range(4):
            key = short_conv(projected, halo, short_filters, 1, jb, cols)
            value = short_conv(projected, halo, short_filters, 2, jb, cols)
            product = key * value
            gated[jb * 128 : jb * 128 + 128, cols] = product
            gated_t[jb, cols, :] = product.T
        return carry

    lax.fori_loop(0, 8, gate, 0)

    def send_group(group, carry):
        def slab(device):
            return pl.ds(pl.multiple_of(device * OWN + group * GROUP, GROUP), GROUP)

        send_slabs(
            gated_t, signal.at[group], slab, pl.ds(pl.multiple_of(me * GROUP, GROUP), GROUP),
            me, tp, signal_send, signal_recv.at[group],
        )
        return carry

    lax.fori_loop(0, GROUPS, send_group, 0)

    def query(cb, carry):
        cols = pl.ds(pl.multiple_of(cb * 128, 128), 128)
        for jb in range(4):
            shortened_q[jb * 128 : jb * 128 + 128, cols] = short_conv(
                projected, halo, short_filters, 0, jb, cols
            )
        return carry

    lax.fori_loop(0, 8, query, 0)

    cosine, sine = twist[0], twist[1]

    def forward(load_block):
        for i in range(GROUP):
            blocks = [load_block(i, jb) for jb in range(4)]
            high, low = split(
                jnp.concatenate(
                    [jnp.concatenate(blocks[:2], 1), jnp.concatenate(blocks[2:], 1)], 0
                )
            )
            turned = dot(first[...], jnp.concatenate([high, low, high], 0))
            real, imag = turned[:64], turned[64:]
            real_high, real_low = split(real * cosine + imag * sine)
            imag_high, imag_low = split(imag * cosine - real * sine)
            rows[i * 64 : i * 64 + 64, :] = jnp.concatenate(
                [real_high, imag_high, real_low, imag_low, real_high, imag_high], 1
            )
        return dot(rows[...], second[...])

    def group_rows(group):
        return pl.ds(pl.multiple_of(group * GROUP * 64, GROUP * 64), GROUP * 64)

    def filter_step(group, carry):
        spectrum[group_rows(group), :] = forward(
            lambda i, jb: filt[jb, pl.ds(group * GROUP + i, CTX, stride=OWN), :]
        )
        return carry

    wait_arrived(filt, filt_recv)
    lax.fori_loop(0, GROUPS, filter_step, 0)

    def signal_step(group, carry):
        wait_arrived(signal.at[group], signal_recv.at[group])
        left = forward(lambda i, jb: signal[group, jb, pl.ds(i, CTX, stride=GROUP), :])
        right = spectrum[group_rows(group), :]
        left_real, left_imag = left[:, :256], left[:, 256:]
        right_real, right_imag = right[:, :256], right[:, 256:]
        real_high, real_low = split(left_real * right_real - left_imag * right_imag)
        imag_high, imag_low = split(left_real * right_imag + left_imag * right_real)
        product = jnp.concatenate(
            [real_high, imag_high, real_low, imag_low, real_high, imag_high], 1
        )
        spectrum[group_rows(group), :] = dot(product, back_second[...])
        return carry

    lax.fori_loop(0, GROUPS, signal_step, 0)
    wait_sent(filt_t, filt_send)

    def back(half):
        lanes = slice(128 * half, 128 * half + 128)
        imag_lanes = slice(256 + 128 * half, 384 + 128 * half)
        cosine, sine = twist[0, :, lanes], twist[1, :, lanes]

        def step(group, carry):
            for i in range(GROUP):
                channel = group * GROUP + i
                block = pl.ds(pl.multiple_of(channel * 64, 64), 64)
                real, imag = spectrum[block, lanes], spectrum[block, imag_lanes]
                real_high, real_low = split(real * cosine - imag * sine)
                imag_high, imag_low = split(imag * cosine + real * sine)
                result = dot(
                    back_first[...],
                    jnp.concatenate(
                        [real_high, imag_high, real_low, imag_low, real_high, imag_high], 0
                    ),
                )
                conv[half, pl.ds(channel, CTX, stride=OWN), :] = result[:32]
                conv[half + 2, pl.ds(channel, CTX, stride=OWN), :] = result[32:]
            return carry

        lax.fori_loop(0, GROUPS, step, 0)
        for jb in (half, half + 2):
            chunk = pl.ds(jb, 1)
            send_slabs(
                conv.at[chunk], conv_in.at[chunk], rows_of, rows_of(me),
                me, tp, conv_send.at[jb], conv_recv.at[jb],
            )

    back(0)
    back(1)
    load_weight.wait()

    def columns(quarter):
        return pl.ds(pl.multiple_of(quarter * 1024, 1024), 1024)

    def to_far(jb, side):
        half = slice(512 * side, 512 * side + 512)
        return pltpu.make_async_remote_copy(
            src_ref=far.at[jb, :, half],
            dst_ref=far_in.at[jb, :, half],
            send_sem=far_send.at[jb, side],
            recv_sem=far_recv.at[jb, side],
            device_id=(me, (up, down)[side]),
            device_id_type=MESH,
        )

    def to_near(jb, side):
        return pltpu.make_async_remote_copy(
            src_ref=near.at[jb, side],
            dst_ref=near_in.at[jb, side],
            send_sem=near_send.at[jb, side],
            recv_sem=near_recv.at[jb, side],
            device_id=(me, (up, down)[side]),
            device_id_type=MESH,
        )

    def compute(jb):
        wait_arrived(conv_in.at[pl.ds(jb, 1)], conv_recv.at[jb])
        tokens = slice(jb * 128, jb * 128 + 128)
        mixed = conv_in[jb].T + skip_gain[...] * gated[tokens, :]
        gated_out[...] = (shortened_q[tokens, :] * mixed).astype(BF16)
        far[jb] = dot(gated_out[...], weight[:, columns(lax.rem(tp + 2, TP))])
        to_far(jb, 0).start()
        to_far(jb, 1).start()
        near[jb, 0] = dot(gated_out[...], weight[:, columns(up)])
        near[jb, 1] = dot(gated_out[...], weight[:, columns(down)])
        out[tokens, :] = dot(gated_out[...], weight[:, columns(tp)])

    def relay(jb):
        for side in (0, 1):
            half = slice(512 * side, 512 * side + 512)
            to_far(jb, side).wait_recv()
            near[jb, side, :, half] += far_in[jb, :, half]
            to_near(jb, side).start()

    order = (0, 2, 1, 3)
    compute(order[0])
    for step in range(1, 4):
        compute(order[step])
        relay(order[step - 1])
    relay(order[3])
    for jb in order:
        tokens = slice(jb * 128, jb * 128 + 128)
        to_near(jb, 0).wait_recv()
        to_near(jb, 1).wait_recv()
        out[tokens, :] += near_in[jb, 0] + near_in[jb, 1]
    wait_sent(gated_t, signal_send)
    for jb in range(4):
        wait_sent(conv.at[pl.ds(jb, 1)], conv_send.at[jb])
        for side in (0, 1):
            to_far(jb, side).wait_send()
            to_near(jb, side).wait_send()


VMEM = pl.BlockSpec(memory_space=pltpu.VMEM)
ANY = pl.BlockSpec(memory_space=pl.ANY)
DMA = pltpu.SemaphoreType.DMA


def per_device(projected, short_filters, long_filter, skip_gain, out_weight):
    return pl.pallas_call(
        mixer_kernel,
        out_shape=jax.ShapeDtypeStruct((512, 1024), F32),
        in_specs=[ANY, VMEM, ANY, VMEM, ANY] + [VMEM] * 5,
        out_specs=VMEM,
        scratch_shapes=[
            pltpu.VMEM((3, 512, 1024), F32),
            pltpu.VMEM((512, 1024), F32),
            pltpu.VMEM((1024, 4096), BF16),
            pltpu.VMEM((3, 8, 1024), F32),
            pltpu.VMEM((3, 8, 1024), F32),
            pltpu.VMEM((4, 1024, 128), F32),
            pltpu.VMEM((4, 1024, 128), F32),
            pltpu.VMEM((4, 1024, 128), F32),
            pltpu.VMEM((GROUPS, 4, CTX * GROUP, 128), F32),
            pltpu.VMEM((512, 1024), F32),
            pltpu.VMEM((512, 1024), F32),
            pltpu.VMEM((GROUP * 64, 1536), BF16),
            pltpu.VMEM((OWN * 64, 512), F32),
            pltpu.VMEM((4, 1024, 128), F32),
            pltpu.VMEM((128, 1024), BF16),
            pltpu.VMEM((4, 128, 1024), F32),
            pltpu.VMEM((4, 2, 128, 1024), F32),
            pltpu.VMEM((4, 128, 1024), F32),
            pltpu.VMEM((4, 2, 128, 1024), F32),
            DMA((3,)),
            DMA,
            DMA,
            DMA,
            DMA,
            DMA,
            DMA((GROUPS,)),
            DMA((4,)),
            DMA((4,)),
            DMA((4, 2)),
            DMA((4, 2)),
            DMA((4, 2)),
            DMA((4, 2)),
        ],
        compiler_params=pltpu.CompilerParams(
            collective_id=0, has_side_effects=True, vmem_limit_bytes=60 * 2**20
        ),
        name="mixer",
    )(
        projected, short_filters, long_filter, skip_gain[None], out_weight,
        *[jnp.asarray(table) for table in tables()],
    )


def solution(mesh):
    return jax.shard_map(
        per_device,
        mesh=mesh,
        in_specs=(
            P(None, "ctx", "tp"),
            P(None, None, "tp"),
            P("ctx", "tp"),
            P("tp"),
            P("tp", None),
        ),
        out_specs=P("ctx", "tp"),
        check_vma=False,
    )
```

```python
import jax
import jax.numpy as jnp
import ml_dtypes
import numpy as np
from jax import lax
from jax.experimental import pallas as pl
from jax.experimental.pallas import tpu as pltpu
from jax.sharding import PartitionSpec as P

MESH = pl.DeviceIdType.MESH
BF16 = jnp.bfloat16
F32 = jnp.float32
CTX = 32
TP = 4
OWN = 32
GROUP = 8
GROUPS = OWN // GROUP
CHIP_OFFSETS = (
    (1, 0), (3, 0), (0, 1), (0, 3), (1, 1), (3, 3), (1, 3), (3, 1),
    (2, 0), (0, 2), (2, 1), (2, 3), (1, 2), (3, 2), (2, 2),
)
PEERS = tuple((a, b, d) for a, b in CHIP_OFFSETS for d in (0, 1)) + ((0, 0, 1),)


def split_np(table):
    high = table.astype(ml_dtypes.bfloat16)
    low = (table - high.astype(np.float64)).astype(ml_dtypes.bfloat16)
    return high, low


def tables():
    block = np.arange(32)
    n1 = np.concatenate([2 * block, 2 * block + 1]).astype(np.float64)
    k1 = np.arange(64) + 0.25
    n2 = np.arange(256)
    psi = 2 * np.pi * np.outer(k1, n1) / 64
    high, low = split_np(np.concatenate([np.cos(psi), -np.sin(psi)], 0))
    first = np.concatenate([high, high, low], 1)
    phi = 2 * np.pi * np.outer(k1, n2) / 16384
    twist = np.stack([np.cos(phi), np.sin(phi)]).astype(np.float32)
    theta = 2 * np.pi * (np.outer(n2, n2) % 256) / 256
    cosine, sine = np.cos(theta), np.sin(theta)
    high, low = split_np(np.block([[cosine, -sine], [sine, cosine]]))
    second = np.concatenate([high, high, low], 0)
    high, low = split_np(np.block([[cosine, sine], [-sine, cosine]]))
    back_second = np.concatenate([high, high, low], 0)
    high, low = split_np(np.concatenate([np.cos(psi.T), -np.sin(psi.T)], 1) / 16384)
    back_first = np.concatenate([high, high, low], 1)
    return first, twist, second, back_second, back_first


def split(value):
    high = value.astype(BF16)
    return high, (value - high.astype(F32)).astype(BF16)


def dot(left, right):
    return jnp.dot(left, right, preferred_element_type=F32)


def ctx_peer(me, offset):
    a, b, d = offset
    return (me // 8 + a) % 4 * 8 + (me // 2 + b) % 4 * 2 + (me + d) % 2


def rows_of(device):
    return pl.ds(pl.multiple_of(device * OWN, OWN), OWN)


def send_slabs(source, target, slab, own_slab, me, tp, send_sem, recv_sem):
    pltpu.make_async_copy(
        source.at[:, slab(me), :], target.at[:, own_slab, :], recv_sem
    ).start()
    for offset in PEERS:
        peer = ctx_peer(me, offset)
        pltpu.make_async_remote_copy(
            src_ref=source.at[:, slab(peer), :],
            dst_ref=target.at[:, own_slab, :],
            send_sem=send_sem,
            recv_sem=recv_sem,
            device_id=(peer, tp),
            device_id_type=MESH,
        ).start()


def wait_arrived(target, recv_sem):
    pltpu.make_async_copy(target, target, recv_sem).wait()


def wait_sent(source, send_sem):
    away = source.at[:, 0 : (CTX - 1) * OWN, :]
    pltpu.make_async_copy(away, away, send_sem).wait()


def short_conv(projected, halo, short_filters, stream, jb, cols):
    rows = projected[stream, jb * 128 : jb * 128 + 128, cols]
    before = halo[stream, :, cols] if jb == 0 else projected[stream, jb * 128 - 8 : jb * 128, cols]
    longer = jnp.concatenate([before, rows], 0)
    taps = short_filters[stream, :, cols]
    return taps[0:1] * rows + taps[1:2] * longer[7:135] + taps[2:3] * longer[6:134]


def mixer_kernel(
    projected_hbm, short_filters, long_filter_hbm, skip_gain, weight_hbm,
    first_hbm, twist_hbm, second_hbm, back_second_hbm, back_first_hbm,
    out,
    projected, long_filter, weight, first, twist, second, back_second, back_first,
    halo, halo_in, filt_t, gated_t, filt, signal,
    shortened_q, rows, spectrum, conv_in, gated_out, far_in, near_in,
    load_sem, halo_send, halo_recv, filt_send, filt_recv, signal_send, signal_recv,
    conv_send, conv_recv, far_send, far_recv, near_send, near_recv,
):
    me = lax.axis_index("ctx")
    tp = lax.axis_index("tp")
    up, down = lax.rem(tp + 1, TP), lax.rem(tp + TP - 1, TP)
    conv = filt_t
    gated = long_filter

    def far(jb):
        return projected.at[0, pl.ds(jb * 128, 128), :]

    def near(jb, side):
        return projected.at[1 + side, pl.ds(jb * 128, 128), :]

    barrier = pltpu.get_barrier_semaphore()

    def signal_peer(i, carry):
        pl.semaphore_signal(
            barrier, inc=1, device_id=(lax.rem(me + i, CTX), tp), device_id_type=MESH
        )
        return carry

    lax.fori_loop(1, CTX, signal_peer, 0)
    for side in (up, down):
        pl.semaphore_signal(barrier, inc=1, device_id=(me, side), device_id_type=MESH)
    load_filter = pltpu.make_async_copy(long_filter_hbm, long_filter, load_sem.at[0])
    load_filter.start()
    load_projected = pltpu.make_async_copy(projected_hbm, projected, load_sem.at[1])
    load_projected.start()
    load_filter.wait()

    def turn_filter(cb, carry):
        cols = pl.ds(pl.multiple_of(cb * 128, 128), 128)
        for jb in range(4):
            filt_t[jb, cols, :] = long_filter[jb * 128 : jb * 128 + 128, cols].T
        return carry

    lax.fori_loop(0, 8, turn_filter, 0)
    pl.semaphore_wait(barrier, CTX + 1)

    edge = pltpu.make_async_remote_copy(
        src_ref=projected_hbm.at[:, 504:512, :],
        dst_ref=halo_in,
        send_sem=halo_send,
        recv_sem=halo_recv,
        device_id=(lax.rem(me + 1, CTX), tp),
        device_id_type=MESH,
    )
    edge.start()
    for half in range(2):
        part = pl.ds(2 * half, 2)
        send_slabs(
            filt_t.at[part], filt.at[part], rows_of, rows_of(me), me, tp, filt_send, filt_recv
        )
    load_projected.wait()
    load_tables = [
        pltpu.make_async_copy(source, target, load_sem.at[3 + i])
        for i, (source, target) in enumerate(
            (
                (first_hbm, first), (twist_hbm, twist), (second_hbm, second),
                (back_second_hbm, back_second), (back_first_hbm, back_first),
            )
        )
    ]
    for load in load_tables:
        load.start()
    load_weight = pltpu.make_async_copy(weight_hbm, weight, load_sem.at[2])
    load_weight.start()
    edge.wait()
    halo[...] = jnp.where(me > 0, halo_in[...], 0.0)

    def gate(cb, carry):
        cols = pl.ds(pl.multiple_of(cb * 128, 128), 128)
        for jb in range(4):
            key = short_conv(projected, halo, short_filters, 1, jb, cols)
            value = short_conv(projected, halo, short_filters, 2, jb, cols)
            product = key * value
            gated[jb * 128 : jb * 128 + 128, cols] = product
            gated_t[jb, cols, :] = product.T
        return carry

    lax.fori_loop(0, 8, gate, 0)

    def send_group(group, carry):
        def slab(device):
            return pl.ds(pl.multiple_of(device * OWN + group * GROUP, GROUP), GROUP)

        send_slabs(
            gated_t, signal.at[group], slab, pl.ds(pl.multiple_of(me * GROUP, GROUP), GROUP),
            me, tp, signal_send, signal_recv.at[group],
        )
        return carry

    lax.fori_loop(0, GROUPS, send_group, 0)

    def query(cb, carry):
        cols = pl.ds(pl.multiple_of(cb * 128, 128), 128)
        for jb in range(4):
            shortened_q[jb * 128 : jb * 128 + 128, cols] = short_conv(
                projected, halo, short_filters, 0, jb, cols
            )
        return carry

    lax.fori_loop(0, 8, query, 0)

    for load in load_tables:
        load.wait()
    cosine, sine = twist[0], twist[1]

    def forward(load_block):
        for i in range(GROUP):
            blocks = [load_block(i, jb) for jb in range(4)]
            high, low = split(
                jnp.concatenate(
                    [jnp.concatenate(blocks[:2], 1), jnp.concatenate(blocks[2:], 1)], 0
                )
            )
            turned = dot(first[...], jnp.concatenate([high, low, high], 0))
            real, imag = turned[:64], turned[64:]
            real_high, real_low = split(real * cosine + imag * sine)
            imag_high, imag_low = split(imag * cosine - real * sine)
            rows[i * 64 : i * 64 + 64, :] = jnp.concatenate(
                [real_high, imag_high, real_low, imag_low, real_high, imag_high], 1
            )
        return dot(rows[...], second[...])

    def group_rows(group):
        return pl.ds(pl.multiple_of(group * GROUP * 64, GROUP * 64), GROUP * 64)

    def filter_step(group, carry):
        spectrum[group_rows(group), :] = forward(
            lambda i, jb: filt[jb, pl.ds(group * GROUP + i, CTX, stride=OWN), :]
        )
        return carry

    wait_arrived(filt, filt_recv)
    lax.fori_loop(0, GROUPS, filter_step, 0)

    def signal_step(group, carry):
        wait_arrived(signal.at[group], signal_recv.at[group])
        left = forward(lambda i, jb: signal[group, jb, pl.ds(i, CTX, stride=GROUP), :])
        right = spectrum[group_rows(group), :]
        left_real, left_imag = left[:, :256], left[:, 256:]
        right_real, right_imag = right[:, :256], right[:, 256:]
        real_high, real_low = split(left_real * right_real - left_imag * right_imag)
        imag_high, imag_low = split(left_real * right_imag + left_imag * right_real)
        product = jnp.concatenate(
            [real_high, imag_high, real_low, imag_low, real_high, imag_high], 1
        )
        spectrum[group_rows(group), :] = dot(product, back_second[...])
        back(0, group)
        return carry

    def back(half, group):
        lanes = slice(128 * half, 128 * half + 128)
        imag_lanes = slice(256 + 128 * half, 384 + 128 * half)
        cosine, sine = twist[0, :, lanes], twist[1, :, lanes]
        for i in range(GROUP):
            channel = group * GROUP + i
            block = pl.ds(pl.multiple_of(channel * 64, 64), 64)
            real, imag = spectrum[block, lanes], spectrum[block, imag_lanes]
            real_high, real_low = split(real * cosine - imag * sine)
            imag_high, imag_low = split(imag * cosine + real * sine)
            result = dot(
                back_first[...],
                jnp.concatenate(
                    [real_high, imag_high, real_low, imag_low, real_high, imag_high], 0
                ),
            )
            conv[half, pl.ds(channel, CTX, stride=OWN), :] = result[:32]
            conv[half + 2, pl.ds(channel, CTX, stride=OWN), :] = result[32:]

    def back_step(group, carry):
        back(1, group)
        return carry

    def return_half(half):
        for jb in (half, half + 2):
            chunk = pl.ds(jb, 1)
            send_slabs(
                conv.at[chunk], conv_in.at[chunk], rows_of, rows_of(me),
                me, tp, conv_send.at[jb], conv_recv.at[jb],
            )

    wait_sent(filt_t, filt_send)
    lax.fori_loop(0, GROUPS, signal_step, 0)
    return_half(0)
    lax.fori_loop(0, GROUPS, back_step, 0)
    return_half(1)
    load_weight.wait()

    def columns(quarter):
        return pl.ds(pl.multiple_of(quarter * 1024, 1024), 1024)

    def to_far(jb, side):
        half = slice(512 * side, 512 * side + 512)
        return pltpu.make_async_remote_copy(
            src_ref=far(jb).at[:, half],
            dst_ref=far_in.at[jb, :, half],
            send_sem=far_send.at[jb, side],
            recv_sem=far_recv.at[jb, side],
            device_id=(me, (up, down)[side]),
            device_id_type=MESH,
        )

    def to_near(jb, side):
        return pltpu.make_async_remote_copy(
            src_ref=near(jb, side),
            dst_ref=near_in.at[jb, side],
            send_sem=near_send.at[jb, side],
            recv_sem=near_recv.at[jb, side],
            device_id=(me, (up, down)[side]),
            device_id_type=MESH,
        )

    def compute(jb):
        wait_arrived(conv_in.at[pl.ds(jb, 1)], conv_recv.at[jb])
        tokens = slice(jb * 128, jb * 128 + 128)
        mixed = conv_in[jb].T + skip_gain[...] * gated[tokens, :]
        gated_out[...] = (shortened_q[tokens, :] * mixed).astype(BF16)
        far(jb)[...] = dot(gated_out[...], weight[:, columns(lax.rem(tp + 2, TP))])
        to_far(jb, 0).start()
        to_far(jb, 1).start()
        near(jb, 0)[...] = dot(gated_out[...], weight[:, columns(up)])
        near(jb, 1)[...] = dot(gated_out[...], weight[:, columns(down)])
        out[tokens, :] = dot(gated_out[...], weight[:, columns(tp)])

    def relay(jb):
        for side in (0, 1):
            half = slice(512 * side, 512 * side + 512)
            to_far(jb, side).wait_recv()
            near(jb, side)[:, half] += far_in[jb, :, half]
            to_near(jb, side).start()

    order = (0, 2, 1, 3)
    compute(order[0])
    for step in range(1, 4):
        compute(order[step])
        relay(order[step - 1])
    relay(order[3])
    for jb in order:
        tokens = slice(jb * 128, jb * 128 + 128)
        to_near(jb, 0).wait_recv()
        to_near(jb, 1).wait_recv()
        out[tokens, :] += near_in[jb, 0] + near_in[jb, 1]
    wait_sent(gated_t, signal_send)
    for jb in range(4):
        wait_sent(conv.at[pl.ds(jb, 1)], conv_send.at[jb])
        for side in (0, 1):
            to_far(jb, side).wait_send()
            to_near(jb, side).wait_send()


VMEM = pl.BlockSpec(memory_space=pltpu.VMEM)
HBM = pl.BlockSpec(memory_space=pltpu.HBM)
DMA = pltpu.SemaphoreType.DMA


def per_device(projected, short_filters, long_filter, skip_gain, out_weight):
    return pl.pallas_call(
        mixer_kernel,
        out_shape=jax.ShapeDtypeStruct((512, 1024), F32),
        in_specs=[HBM, VMEM, HBM, VMEM, HBM] + [HBM] * 5,
        out_specs=VMEM,
        scratch_shapes=[
            pltpu.VMEM((3, 512, 1024), F32),
            pltpu.VMEM((512, 1024), F32),
            pltpu.VMEM((1024, 4096), BF16),
            pltpu.VMEM((128, 192), BF16),
            pltpu.VMEM((2, 64, 256), F32),
            pltpu.VMEM((1536, 512), BF16),
            pltpu.VMEM((1536, 512), BF16),
            pltpu.VMEM((64, 384), BF16),
            pltpu.VMEM((3, 8, 1024), F32),
            pltpu.VMEM((3, 8, 1024), F32),
            pltpu.VMEM((4, 1024, 128), F32),
            pltpu.VMEM((4, 1024, 128), F32),
            pltpu.VMEM((4, 1024, 128), F32),
            pltpu.VMEM((GROUPS, 4, CTX * GROUP, 128), F32),
            pltpu.VMEM((512, 1024), F32),
            pltpu.VMEM((GROUP * 64, 1536), BF16),
            pltpu.VMEM((OWN * 64, 512), F32),
            pltpu.VMEM((4, 1024, 128), F32),
            pltpu.VMEM((128, 1024), BF16),
            pltpu.VMEM((4, 128, 1024), F32),
            pltpu.VMEM((4, 2, 128, 1024), F32),
            DMA((8,)),
            DMA,
            DMA,
            DMA,
            DMA,
            DMA,
            DMA((GROUPS,)),
            DMA((4,)),
            DMA((4,)),
            DMA((4, 2)),
            DMA((4, 2)),
            DMA((4, 2)),
            DMA((4, 2)),
        ],
        compiler_params=pltpu.CompilerParams(
            collective_id=0, has_side_effects=True, vmem_limit_bytes=60 * 2**20
        ),
        name="mixer",
    )(
        projected, short_filters, long_filter, skip_gain[None], out_weight,
        *[jnp.asarray(table) for table in tables()],
    )


def solution(mesh):
    return jax.shard_map(
        per_device,
        mesh=mesh,
        in_specs=(
            P(None, "ctx", "tp"),
            P(None, None, "tp"),
            P("ctx", "tp"),
            P("tp"),
            P("tp", None),
        ),
        out_specs=P("ctx", "tp"),
        check_vma=False,
    )
```

```python
import jax
import jax.numpy as jnp
import ml_dtypes
import numpy as np
from jax import lax
from jax.experimental import pallas as pl
from jax.experimental.pallas import tpu as pltpu
from jax.sharding import PartitionSpec as P

MESH = pl.DeviceIdType.MESH
BF16 = jnp.bfloat16
F32 = jnp.float32
CTX = 32
TP = 4
OWN = 32
GROUP = 8
GROUPS = OWN // GROUP
CHIP_OFFSETS = (
    (1, 0), (3, 0), (0, 1), (0, 3), (1, 1), (3, 3), (1, 3), (3, 1),
    (2, 0), (0, 2), (2, 1), (2, 3), (1, 2), (3, 2), (2, 2),
)
PEERS = tuple((a, b, d) for a, b in CHIP_OFFSETS for d in (0, 1)) + ((0, 0, 1),)


def split_np(table):
    high = table.astype(ml_dtypes.bfloat16)
    low = (table - high.astype(np.float64)).astype(ml_dtypes.bfloat16)
    return high, low


def tables():
    block = np.arange(32)
    n1 = np.concatenate([2 * block, 2 * block + 1]).astype(np.float64)
    k1 = np.arange(64) + 0.25
    n2 = np.arange(256)
    psi = 2 * np.pi * np.outer(k1, n1) / 64
    high, low = split_np(np.concatenate([np.cos(psi), -np.sin(psi)], 0))
    first = np.concatenate([high, high, low], 1)
    phi = 2 * np.pi * np.outer(k1, n2) / 16384
    twist = np.stack([np.cos(phi), np.sin(phi)]).astype(np.float32)
    theta = 2 * np.pi * (np.outer(n2, n2) % 256) / 256
    cosine, sine = np.cos(theta), np.sin(theta)
    high, low = split_np(np.block([[cosine, -sine], [sine, cosine]]))
    second = np.concatenate([high, high, low], 0)
    high, low = split_np(np.block([[cosine, sine], [-sine, cosine]]))
    back_second = np.concatenate([high, high, low], 0)
    high, low = split_np(np.concatenate([np.cos(psi.T), -np.sin(psi.T)], 1) / 16384)
    back_first = np.concatenate([high, high, low], 1)
    return first, twist, second, back_second, back_first


def split(value):
    high = value.astype(BF16)
    return high, (value - high.astype(F32)).astype(BF16)


def dot(left, right):
    return jnp.dot(left, right, preferred_element_type=F32)


def ctx_peer(me, offset):
    a, b, d = offset
    return (me // 8 + a) % 4 * 8 + (me // 2 + b) % 4 * 2 + (me + d) % 2


def rows_of(device):
    return pl.ds(pl.multiple_of(device * OWN, OWN), OWN)


def send_slabs(source, target, slab, own_slab, me, tp, send_sem, recv_sem):
    pltpu.make_async_copy(
        source.at[:, slab(me), :], target.at[:, own_slab, :], recv_sem
    ).start()
    for offset in PEERS:
        peer = ctx_peer(me, offset)
        pltpu.make_async_remote_copy(
            src_ref=source.at[:, slab(peer), :],
            dst_ref=target.at[:, own_slab, :],
            send_sem=send_sem,
            recv_sem=recv_sem,
            device_id=(peer, tp),
            device_id_type=MESH,
        ).start()


def wait_arrived(target, recv_sem):
    pltpu.make_async_copy(target, target, recv_sem).wait()


def wait_sent(source, send_sem):
    away = source.at[:, 0 : (CTX - 1) * OWN, :]
    pltpu.make_async_copy(away, away, send_sem).wait()


def short_conv(projected, halo, short_filters, stream, jb, cols):
    rows = projected[stream, jb * 128 : jb * 128 + 128, cols]
    before = halo[stream, :, cols] if jb == 0 else projected[stream, jb * 128 - 8 : jb * 128, cols]
    longer = jnp.concatenate([before, rows], 0)
    taps = short_filters[stream, :, cols]
    return taps[0:1] * rows + taps[1:2] * longer[7:135] + taps[2:3] * longer[6:134]


def mixer_kernel(
    projected_hbm, short_filters, long_filter_hbm, skip_gain, weight_hbm,
    first_hbm, twist_hbm, second_hbm, back_second_hbm, back_first_hbm,
    out,
    projected, long_filter, weight, first, twist, second, back_second, back_first,
    halo, halo_in, filt_t, gated_t, filt, signal,
    shortened_q, rows, spectrum, conv_in, gated_out, partner_out, weight_in, partner_weight,
    gather_in, sum_in, near_in_partner,
    load_sem, halo_send, halo_recv, filt_send, filt_recv, signal_send, signal_recv,
    conv_send, conv_recv, fetch_send, fetch_recv, share_send, share_recv, swap_send, swap_recv,
    gather_send, gather_recv, sum_send, sum_recv, far_send, far_recv, near_send, near_recv,
):
    me = lax.axis_index("ctx")
    tp = lax.axis_index("tp")
    partner, mate = tp + 1 - 2 * (tp % 2), TP - 1 - tp
    parity = (me // 8 + me // 2) % 2
    mine, theirs = 2 * parity + me % 2, 2 * (1 - parity) + me % 2
    conv = filt_t
    gated = long_filter
    fetch_out = out

    def sum_out(jb):
        return projected.at[0, pl.ds(jb * 128, 128), :]

    def gather_out(jb):
        return projected.at[1, pl.ds(jb * 128, 128), :]

    far = projected.at[0, pl.ds(0, 128), :]
    near = (projected.at[1, pl.ds(0, 128), :], projected.at[2, pl.ds(0, 128), :])
    far_in, near_in = gather_in.at[0], (sum_in.at[0], near_in_partner)

    def columns(quarter):
        return pl.ds(pl.multiple_of(quarter * 1024, 1024), 1024)

    def quarter_rows(quarter):
        return pl.ds(pl.multiple_of(quarter * 256, 256), 256)

    def to_tp(source, target, device, send_sem, recv_sem):
        return pltpu.make_async_remote_copy(
            src_ref=source,
            dst_ref=target,
            send_sem=send_sem,
            recv_sem=recv_sem,
            device_id=(me, device),
            device_id_type=MESH,
        )

    def fetch(part):
        return to_tp(
            fetch_out.at[pl.ds(part * 256, 256), :],
            weight_in.at[quarter_rows(mine), pl.ds(part * 1024, 1024)],
            partner, fetch_send.at[part], fetch_recv.at[part],
        )

    def share(part):
        for direction, offset in enumerate(((1, 0, 0), (3, 0, 0), (0, 1, 0), (0, 3, 0))):
            first_row = mine * 256 + direction * 64 + part * 32
            slab = weight_in.at[pl.ds(pl.multiple_of(first_row, 32), 32), :]
            pltpu.make_async_remote_copy(
                src_ref=slab,
                dst_ref=slab,
                send_sem=share_send.at[part],
                recv_sem=share_recv.at[part],
                device_id=(ctx_peer(me, offset), tp),
                device_id_type=MESH,
            ).start()

    def share_bytes():
        return weight_in.at[pl.ds(pl.multiple_of(theirs * 256, 256), 128), :]

    def swap(which):
        slab = weight_in.at[quarter_rows((mine, theirs)[which]), :]
        return pltpu.make_async_remote_copy(
            src_ref=slab,
            dst_ref=slab,
            send_sem=swap_send.at[which],
            recv_sem=swap_recv.at[which],
            device_id=(ctx_peer(me, (0, 0, 1)), tp),
            device_id_type=MESH,
        )

    def round_quarters(which):
        first_row = ((parity, 1 - parity)[which]) * 512

        def step(i, carry):
            block = pl.ds(pl.multiple_of(first_row + i * 64, 64), 64)
            partner_weight[block, :] = weight_in[block, :].astype(BF16)
            return carry

        lax.fori_loop(0, 8, step, 0)

    barrier = pltpu.get_barrier_semaphore()

    def signal_peer(i, carry):
        pl.semaphore_signal(
            barrier, inc=1, device_id=(lax.rem(me + i, CTX), tp), device_id_type=MESH
        )
        return carry

    lax.fori_loop(1, CTX, signal_peer, 0)
    for side in (partner, mate):
        pl.semaphore_signal(barrier, inc=1, device_id=(me, side), device_id_type=MESH)
    load_filter = pltpu.make_async_copy(long_filter_hbm, long_filter, load_sem.at[0])
    load_filter.start()
    load_projected = pltpu.make_async_copy(projected_hbm, projected, load_sem.at[1])
    load_projected.start()
    load_weight = [
        pltpu.make_async_copy(
            weight_hbm.at[quarter_rows(lax.rem(mine + i, 4)), :],
            weight.at[quarter_rows(lax.rem(mine + i, 4)), :],
            load_sem.at[8 + i],
        )
        for i in range(4)
    ]
    load_weight[0].start()
    load_filter.wait()

    def turn_filter(cb, carry):
        cols = pl.ds(pl.multiple_of(cb * 128, 128), 128)
        for jb in range(4):
            filt_t[jb, cols, :] = long_filter[jb * 128 : jb * 128 + 128, cols].T
        return carry

    lax.fori_loop(0, 8, turn_filter, 0)
    load_weight[0].wait()
    for part, quarter in enumerate((partner, TP - 1 - partner)):
        fetch_out[part * 256 : part * 256 + 256, :] = weight[
            quarter_rows(mine), columns(quarter)
        ].astype(F32)
    pl.semaphore_wait(barrier, CTX + 1)

    edge = pltpu.make_async_remote_copy(
        src_ref=projected_hbm.at[:, 504:512, :],
        dst_ref=halo_in,
        send_sem=halo_send,
        recv_sem=halo_recv,
        device_id=(lax.rem(me + 1, CTX), tp),
        device_id_type=MESH,
    )
    edge.start()
    for half in range(2):
        part = pl.ds(2 * half, 2)
        send_slabs(
            filt_t.at[part], filt.at[part], rows_of, rows_of(me), me, tp, filt_send, filt_recv
        )
    fetch(0).start()
    fetch(1).start()
    load_projected.wait()
    load_tables = [
        pltpu.make_async_copy(source, target, load_sem.at[3 + i])
        for i, (source, target) in enumerate(
            (
                (first_hbm, first), (twist_hbm, twist), (second_hbm, second),
                (back_second_hbm, back_second), (back_first_hbm, back_first),
            )
        )
    ]
    for load in load_tables:
        load.start()
    for load in load_weight[1:]:
        load.start()
    edge.wait()
    halo[...] = jnp.where(me > 0, halo_in[...], 0.0)

    def gate(cb, carry):
        cols = pl.ds(pl.multiple_of(cb * 128, 128), 128)
        for jb in range(4):
            key = short_conv(projected, halo, short_filters, 1, jb, cols)
            value = short_conv(projected, halo, short_filters, 2, jb, cols)
            product = key * value
            gated[jb * 128 : jb * 128 + 128, cols] = product
            gated_t[jb, cols, :] = product.T
        return carry

    lax.fori_loop(0, 8, gate, 0)

    def send_group(group, carry):
        def slab(device):
            return pl.ds(pl.multiple_of(device * OWN + group * GROUP, GROUP), GROUP)

        send_slabs(
            gated_t, signal.at[group], slab, pl.ds(pl.multiple_of(me * GROUP, GROUP), GROUP),
            me, tp, signal_send, signal_recv.at[group],
        )
        return carry

    lax.fori_loop(0, GROUPS, send_group, 0)

    def query(cb, carry):
        cols = pl.ds(pl.multiple_of(cb * 128, 128), 128)
        for jb in range(4):
            shortened_q[jb * 128 : jb * 128 + 128, cols] = short_conv(
                projected, halo, short_filters, 0, jb, cols
            )
        return carry

    lax.fori_loop(0, 8, query, 0)

    for load in load_tables:
        load.wait()
    cosine, sine = twist[0], twist[1]

    def forward(load_block):
        for i in range(GROUP):
            blocks = [load_block(i, jb) for jb in range(4)]
            high, low = split(
                jnp.concatenate(
                    [jnp.concatenate(blocks[:2], 1), jnp.concatenate(blocks[2:], 1)], 0
                )
            )
            turned = dot(first[...], jnp.concatenate([high, low, high], 0))
            real, imag = turned[:64], turned[64:]
            real_high, real_low = split(real * cosine + imag * sine)
            imag_high, imag_low = split(imag * cosine - real * sine)
            rows[i * 64 : i * 64 + 64, :] = jnp.concatenate(
                [real_high, imag_high, real_low, imag_low, real_high, imag_high], 1
            )
        return dot(rows[...], second[...])

    def group_rows(group):
        return pl.ds(pl.multiple_of(group * GROUP * 64, GROUP * 64), GROUP * 64)

    def filter_step(group, carry):
        spectrum[group_rows(group), :] = forward(
            lambda i, jb: filt[jb, pl.ds(group * GROUP + i, CTX, stride=OWN), :]
        )
        return carry

    wait_arrived(filt, filt_recv)
    lax.fori_loop(0, GROUPS, filter_step, 0)

    def signal_step(group, carry):
        left = forward(lambda i, jb: signal[group, jb, pl.ds(i, CTX, stride=GROUP), :])
        right = spectrum[group_rows(group), :]
        left_real, left_imag = left[:, :256], left[:, 256:]
        right_real, right_imag = right[:, :256], right[:, 256:]
        real_high, real_low = split(left_real * right_real - left_imag * right_imag)
        imag_high, imag_low = split(left_real * right_imag + left_imag * right_real)
        product = jnp.concatenate(
            [real_high, imag_high, real_low, imag_low, real_high, imag_high], 1
        )
        spectrum[group_rows(group), :] = dot(product, back_second[...])
        back(0, group)
        return carry

    def back(half, group):
        lanes = slice(128 * half, 128 * half + 128)
        imag_lanes = slice(256 + 128 * half, 384 + 128 * half)
        cosine, sine = twist[0, :, lanes], twist[1, :, lanes]
        for i in range(GROUP):
            channel = group * GROUP + i
            block = pl.ds(pl.multiple_of(channel * 64, 64), 64)
            real, imag = spectrum[block, lanes], spectrum[block, imag_lanes]
            real_high, real_low = split(real * cosine - imag * sine)
            imag_high, imag_low = split(imag * cosine + real * sine)
            result = dot(
                back_first[...],
                jnp.concatenate(
                    [real_high, imag_high, real_low, imag_low, real_high, imag_high], 0
                ),
            )
            conv[half, pl.ds(channel, CTX, stride=OWN), :] = result[:32]
            conv[half + 2, pl.ds(channel, CTX, stride=OWN), :] = result[32:]

    def back_step(group, carry):
        back(1, group)
        return carry

    def return_chunk(jb):
        chunk = pl.ds(jb, 1)
        send_slabs(
            conv.at[chunk], conv_in.at[chunk], rows_of, rows_of(me),
            me, tp, conv_send.at[jb], conv_recv.at[jb],
        )

    wait_sent(filt_t, filt_send)
    def early_step(group, carry):
        wait_arrived(signal.at[group], signal_recv.at[group])
        return signal_step(group, carry)

    lax.fori_loop(0, GROUPS - 1, early_step, 0)
    wait_arrived(signal.at[GROUPS - 1], signal_recv.at[GROUPS - 1])
    for part in range(2):
        fetch(part).wait_recv()
    share(0)
    swap(0).start()
    signal_step(GROUPS - 1, 0)
    return_chunk(0)
    return_chunk(2)
    share(1)
    lax.fori_loop(0, GROUPS, back_step, 0)
    return_chunk(1)
    return_chunk(3)
    for load in load_weight[1:]:
        load.wait()
    for part in range(2):
        fetch(part).wait_send()

    def gather(jb):
        return to_tp(
            gather_out(jb), gather_in.at[jb], partner, gather_send.at[jb], gather_recv.at[jb]
        )

    def send_sum(jb):
        return to_tp(sum_out(jb), sum_in.at[jb], mate, sum_send.at[jb], sum_recv.at[jb])

    def gate_chunk(jb):
        wait_arrived(conv_in.at[pl.ds(jb, 1)], conv_recv.at[jb])
        tokens = slice(jb * 128, jb * 128 + 128)
        mixed = conv_in[jb].T + skip_gain[...] * gated[tokens, :]
        gated_out[jb] = (shortened_q[tokens, :] * mixed).astype(BF16)

    def start_gather(jb):
        gather_out(jb)[...] = gated_out[jb].astype(F32)
        gather(jb).start()

    def project(jb):
        gather(jb).wait_recv()
        partner_out[...] = gather_in[jb].astype(BF16)
        sum_out(jb)[...] = dot(gated_out[jb], weight[:, columns(mate)]) + dot(
            partner_out[...], partner_weight[:, 1024:]
        )
        send_sum(jb).start()
        out[jb * 128 : jb * 128 + 128, :] = dot(gated_out[jb], weight[:, columns(tp)]) + dot(
            partner_out[...], partner_weight[:, :1024]
        )

    def finish(jb):
        send_sum(jb).wait_recv()
        out[jb * 128 : jb * 128 + 128, :] += sum_in[jb]

    halves = (slice(0, 512), slice(512, 1024))

    def to_far(side):
        return to_tp(
            far.at[:, halves[1 - side]], far_in.at[:, halves[1 - side]],
            (mate, partner)[side], far_send.at[side], far_recv.at[side],
        )

    def to_near(side):
        return to_tp(
            near[side], near_in[side], (mate, partner)[side], near_send.at[side], near_recv.at[side]
        )

    def relay(side):
        to_far(1 - side).wait_recv()
        near[side][:, halves[side]] += far_in[:, halves[side]]
        to_near(side).start()

    gate_chunk(0)
    far[...] = dot(gated_out[0], weight[:, columns(lax.rem(tp + 2, TP))])
    to_far(0).start()
    to_far(1).start()
    near[0][...] = dot(gated_out[0], weight[:, columns(mate)])
    near[1][...] = dot(gated_out[0], weight[:, columns(partner)])
    out[0:128, :] = dot(gated_out[0], weight[:, columns(tp)])
    gate_chunk(2)
    start_gather(2)
    relay(0)
    for part in range(2):
        pltpu.make_async_copy(share_bytes(), share_bytes(), share_recv.at[part]).wait()
    swap(1).start()
    swap(0).wait_recv()
    round_quarters(0)
    gate_chunk(1)
    swap(1).wait_recv()
    round_quarters(1)
    gather(2).wait_send()
    start_gather(1)
    project(2)
    gate_chunk(3)
    gather(1).wait_send()
    start_gather(3)
    project(1)
    gather(3).wait_send()
    relay(1)
    project(3)
    finish(2)
    finish(1)
    to_near(0).wait_recv()
    to_near(1).wait_recv()
    out[0:128, :] += near_in[0][...] + near_in[1][...]
    finish(3)
    for side in range(2):
        to_far(side).wait_send()
        to_near(side).wait_send()
    wait_sent(gated_t, signal_send)
    for part in range(2):
        pltpu.make_async_copy(share_bytes(), share_bytes(), share_send.at[part]).wait()
        swap(part).wait_send()
    for jb in range(4):
        wait_sent(conv.at[pl.ds(jb, 1)], conv_send.at[jb])
        if jb:
            send_sum(jb).wait_send()


VMEM = pl.BlockSpec(memory_space=pltpu.VMEM)
HBM = pl.BlockSpec(memory_space=pltpu.HBM)
DMA = pltpu.SemaphoreType.DMA


def per_device(projected, short_filters, long_filter, skip_gain, out_weight):
    return pl.pallas_call(
        mixer_kernel,
        out_shape=jax.ShapeDtypeStruct((512, 1024), F32),
        in_specs=[HBM, VMEM, HBM, VMEM, HBM] + [HBM] * 5,
        out_specs=VMEM,
        scratch_shapes=[
            pltpu.VMEM((3, 512, 1024), F32),
            pltpu.VMEM((512, 1024), F32),
            pltpu.VMEM((1024, 4096), BF16),
            pltpu.VMEM((128, 192), BF16),
            pltpu.VMEM((2, 64, 256), F32),
            pltpu.VMEM((1536, 512), BF16),
            pltpu.VMEM((1536, 512), BF16),
            pltpu.VMEM((64, 384), BF16),
            pltpu.VMEM((3, 8, 1024), F32),
            pltpu.VMEM((3, 8, 1024), F32),
            pltpu.VMEM((4, 1024, 128), F32),
            pltpu.VMEM((4, 1024, 128), F32),
            pltpu.VMEM((4, 1024, 128), F32),
            pltpu.VMEM((GROUPS, 4, CTX * GROUP, 128), F32),
            pltpu.VMEM((512, 1024), F32),
            pltpu.VMEM((GROUP * 64, 1536), BF16),
            pltpu.VMEM((OWN * 64, 512), F32),
            pltpu.VMEM((4, 1024, 128), F32),
            pltpu.VMEM((4, 128, 1024), BF16),
            pltpu.VMEM((128, 1024), BF16),
            pltpu.VMEM((1024, 2048), F32),
            pltpu.VMEM((1024, 2048), BF16),
            pltpu.VMEM((4, 128, 1024), F32),
            pltpu.VMEM((4, 128, 1024), F32),
            pltpu.VMEM((128, 1024), F32),
            DMA((12,)),
            DMA,
            DMA,
            DMA,
            DMA,
            DMA,
            DMA((GROUPS,)),
            DMA((4,)),
            DMA((4,)),
            DMA((2,)),
            DMA((2,)),
            DMA((2,)),
            DMA((2,)),
            DMA((2,)),
            DMA((2,)),
            DMA((4,)),
            DMA((4,)),
            DMA((4,)),
            DMA((4,)),
            DMA((2,)),
            DMA((2,)),
            DMA((2,)),
            DMA((2,)),
        ],
        compiler_params=pltpu.CompilerParams(
            collective_id=0, has_side_effects=True, vmem_limit_bytes=60 * 2**20
        ),
        name="mixer",
    )(
        projected, short_filters, long_filter, skip_gain[None], out_weight,
        *[jnp.asarray(table) for table in tables()],
    )


def solution(mesh):
    return jax.shard_map(
        per_device,
        mesh=mesh,
        in_specs=(
            P(None, "ctx", "tp"),
            P(None, None, "tp"),
            P("ctx", "tp"),
            P("tp"),
            P("tp", None),
        ),
        out_specs=P("ctx", "tp"),
        check_vma=False,
    )
```

```python
import jax
import jax.numpy as jnp
import ml_dtypes
import numpy as np
from jax import lax
from jax.experimental import pallas as pl
from jax.experimental.pallas import tpu as pltpu
from jax.sharding import PartitionSpec as P

MESH = pl.DeviceIdType.MESH
BF16 = jnp.bfloat16
F32 = jnp.float32
CTX = 32
TP = 4
OWN = 32
GROUP = 8
GROUPS = OWN // GROUP
CHIP_OFFSETS = (
    (1, 0), (3, 0), (0, 1), (0, 3), (1, 1), (3, 3), (1, 3), (3, 1),
    (2, 0), (0, 2), (2, 1), (2, 3), (1, 2), (3, 2), (2, 2),
)
PEERS = tuple((a, b, d) for a, b in CHIP_OFFSETS for d in (0, 1)) + ((0, 0, 1),)


def split_np(table):
    high = table.astype(ml_dtypes.bfloat16)
    low = (table - high.astype(np.float64)).astype(ml_dtypes.bfloat16)
    return high, low


def tables():
    block = np.arange(32)
    n1 = np.concatenate([2 * block, 2 * block + 1]).astype(np.float64)
    k1 = np.arange(64) + 0.25
    n2 = np.arange(256)
    psi = 2 * np.pi * np.outer(k1, n1) / 64
    high, low = split_np(np.concatenate([np.cos(psi), -np.sin(psi)], 0))
    first = np.concatenate([high, high, low], 1)
    phi = 2 * np.pi * np.outer(k1, n2) / 16384
    twist = np.stack([np.cos(phi), np.sin(phi)]).astype(np.float32)
    theta = 2 * np.pi * (np.outer(n2, n2) % 256) / 256
    cosine, sine = np.cos(theta), np.sin(theta)
    high, low = split_np(np.block([[cosine, -sine], [sine, cosine]]))
    second = np.concatenate([high, high, low], 0)
    high, low = split_np(np.block([[cosine, sine], [-sine, cosine]]))
    back_second = np.concatenate([high, high, low], 0)
    high, low = split_np(np.concatenate([np.cos(psi.T), -np.sin(psi.T)], 1) / 16384)
    back_first = np.concatenate([high, high, low], 1)
    return first, twist, second, back_second, back_first


def split(value):
    high = value.astype(BF16)
    return high, (value - high.astype(F32)).astype(BF16)


def dot(left, right):
    return jnp.dot(left, right, preferred_element_type=F32)


def ctx_peer(me, offset):
    a, b, d = offset
    return (me // 8 + a) % 4 * 8 + (me // 2 + b) % 4 * 2 + (me + d) % 2


def rows_of(device):
    return pl.ds(pl.multiple_of(device * OWN, OWN), OWN)


def send_slabs(source, target, slab, own_slab, me, tp, send_sem, recv_sem):
    pltpu.make_async_copy(
        source.at[:, slab(me), :], target.at[:, own_slab, :], recv_sem
    ).start()
    for offset in PEERS:
        peer = ctx_peer(me, offset)
        pltpu.make_async_remote_copy(
            src_ref=source.at[:, slab(peer), :],
            dst_ref=target.at[:, own_slab, :],
            send_sem=send_sem,
            recv_sem=recv_sem,
            device_id=(peer, tp),
            device_id_type=MESH,
        ).start()


def wait_arrived(target, recv_sem):
    pltpu.make_async_copy(target, target, recv_sem).wait()


def wait_sent(source, send_sem):
    away = source.at[:, 0 : (CTX - 1) * OWN, :]
    pltpu.make_async_copy(away, away, send_sem).wait()


def short_conv(projected, halo, short_filters, stream, jb, cols):
    rows = projected[stream, jb * 128 : jb * 128 + 128, cols]
    before = halo[stream, :, cols] if jb == 0 else projected[stream, jb * 128 - 8 : jb * 128, cols]
    longer = jnp.concatenate([before, rows], 0)
    taps = short_filters[stream, :, cols]
    return taps[0:1] * rows + taps[1:2] * longer[7:135] + taps[2:3] * longer[6:134]


def mixer_kernel(
    projected_hbm, short_filters, long_filter_hbm, skip_gain, weight_hbm,
    first_hbm, twist_hbm, second_hbm, back_second_hbm, back_first_hbm,
    out,
    projected, long_filter, weight, first, twist, second, back_second, back_first,
    halo, halo_in, filt_t, gated_t, filt, signal,
    shortened_q, rows, spectrum, conv_in, gated_out, partner_out, weight_in, partner_weight,
    gather_in, sum_in, near_in_partner,
    load_sem, halo_send, halo_recv, filt_send, filt_recv, signal_send, signal_recv,
    conv_send, conv_recv, fetch_send, fetch_recv, share_send, share_recv, swap_send, swap_recv,
    gather_send, gather_recv, sum_send, sum_recv, far_send, far_recv, near_send, near_recv,
):
    me = lax.axis_index("ctx")
    tp = lax.axis_index("tp")
    partner, mate = tp + 1 - 2 * (tp % 2), TP - 1 - tp
    parity = (me // 8 + me // 2) % 2
    mine, theirs = 2 * parity + me % 2, 2 * (1 - parity) + me % 2
    conv = filt_t
    gated = long_filter
    fetch_out = out

    def sum_out(jb):
        return projected.at[0, pl.ds(jb * 128, 128), :]

    def gather_out(jb):
        return projected.at[1, pl.ds(jb * 128, 128), :]

    far = projected.at[0, pl.ds(0, 128), :]
    near = (projected.at[1, pl.ds(0, 128), :], projected.at[2, pl.ds(0, 128), :])
    far_in, near_in = gather_in.at[0], (sum_in.at[0], near_in_partner)

    def columns(quarter):
        return pl.ds(pl.multiple_of(quarter * 1024, 1024), 1024)

    def quarter_rows(quarter):
        return pl.ds(pl.multiple_of(quarter * 256, 256), 256)

    def to_tp(source, target, device, send_sem, recv_sem):
        return pltpu.make_async_remote_copy(
            src_ref=source,
            dst_ref=target,
            send_sem=send_sem,
            recv_sem=recv_sem,
            device_id=(me, device),
            device_id_type=MESH,
        )

    def fetch(part):
        return to_tp(
            fetch_out.at[pl.ds(part * 256, 256), :],
            weight_in.at[quarter_rows(mine), pl.ds(part * 1024, 1024)],
            partner, fetch_send.at[part], fetch_recv.at[part],
        )

    def share(part):
        for direction, offset in enumerate(((1, 0, 0), (3, 0, 0), (0, 1, 0), (0, 3, 0))):
            first_row = mine * 256 + part * 128 + direction * 32
            slab = weight_in.at[pl.ds(pl.multiple_of(first_row, 32), 32), :]
            pltpu.make_async_remote_copy(
                src_ref=slab,
                dst_ref=slab,
                send_sem=share_send.at[part],
                recv_sem=share_recv.at[part],
                device_id=(ctx_peer(me, offset), tp),
                device_id_type=MESH,
            ).start()

    def shared(quarter, part):
        return weight_in.at[pl.ds(pl.multiple_of(quarter * 256 + part * 128, 128), 128), :]

    def swap(which):
        slab = weight_in.at[quarter_rows(mine), :] if which == 2 else shared(theirs, which)
        return pltpu.make_async_remote_copy(
            src_ref=slab,
            dst_ref=slab,
            send_sem=swap_send.at[which],
            recv_sem=swap_recv.at[which],
            device_id=(ctx_peer(me, (0, 0, 1)), tp),
            device_id_type=MESH,
        )

    def round_quarters(which):
        first_row = ((parity, 1 - parity)[which]) * 512

        def step(i, carry):
            block = pl.ds(pl.multiple_of(first_row + i * 64, 64), 64)
            partner_weight[block, :] = weight_in[block, :].astype(BF16)
            return carry

        lax.fori_loop(0, 8, step, 0)

    barrier = pltpu.get_barrier_semaphore()

    def signal_peer(i, carry):
        pl.semaphore_signal(
            barrier, inc=1, device_id=(lax.rem(me + i, CTX), tp), device_id_type=MESH
        )
        return carry

    lax.fori_loop(1, CTX, signal_peer, 0)
    for side in (partner, mate):
        pl.semaphore_signal(barrier, inc=1, device_id=(me, side), device_id_type=MESH)
    load_filter = pltpu.make_async_copy(long_filter_hbm, long_filter, load_sem.at[0])
    load_filter.start()
    load_projected = pltpu.make_async_copy(projected_hbm, projected, load_sem.at[1])
    load_projected.start()
    load_weight = [
        pltpu.make_async_copy(
            weight_hbm.at[quarter_rows(lax.rem(mine + i, 4)), :],
            weight.at[quarter_rows(lax.rem(mine + i, 4)), :],
            load_sem.at[8 + i],
        )
        for i in range(4)
    ]
    load_weight[0].start()
    load_filter.wait()

    def turn_filter(cb, carry):
        cols = pl.ds(pl.multiple_of(cb * 128, 128), 128)
        for jb in range(4):
            filt_t[jb, cols, :] = long_filter[jb * 128 : jb * 128 + 128, cols].T
        return carry

    lax.fori_loop(0, 8, turn_filter, 0)
    load_weight[0].wait()
    for part, quarter in enumerate((partner, TP - 1 - partner)):
        fetch_out[part * 256 : part * 256 + 256, :] = weight[
            quarter_rows(mine), columns(quarter)
        ].astype(F32)
    pl.semaphore_wait(barrier, CTX + 1)

    edge = pltpu.make_async_remote_copy(
        src_ref=projected_hbm.at[:, 504:512, :],
        dst_ref=halo_in,
        send_sem=halo_send,
        recv_sem=halo_recv,
        device_id=(lax.rem(me + 1, CTX), tp),
        device_id_type=MESH,
    )
    edge.start()
    for half in range(2):
        part = pl.ds(2 * half, 2)
        send_slabs(
            filt_t.at[part], filt.at[part], rows_of, rows_of(me), me, tp, filt_send, filt_recv
        )
    fetch(0).start()
    fetch(1).start()
    load_projected.wait()
    load_tables = [
        pltpu.make_async_copy(source, target, load_sem.at[3 + i])
        for i, (source, target) in enumerate(
            (
                (first_hbm, first), (twist_hbm, twist), (second_hbm, second),
                (back_second_hbm, back_second), (back_first_hbm, back_first),
            )
        )
    ]
    for load in load_tables:
        load.start()
    for load in load_weight[1:]:
        load.start()
    edge.wait()
    halo[...] = jnp.where(me > 0, halo_in[...], 0.0)

    def gate(cb, carry):
        cols = pl.ds(pl.multiple_of(cb * 128, 128), 128)
        for jb in range(4):
            key = short_conv(projected, halo, short_filters, 1, jb, cols)
            value = short_conv(projected, halo, short_filters, 2, jb, cols)
            product = key * value
            gated[jb * 128 : jb * 128 + 128, cols] = product
            gated_t[jb, cols, :] = product.T
        return carry

    lax.fori_loop(0, 8, gate, 0)

    def send_group(group, carry):
        def slab(device):
            return pl.ds(pl.multiple_of(device * OWN + group * GROUP, GROUP), GROUP)

        send_slabs(
            gated_t, signal.at[group], slab, pl.ds(pl.multiple_of(me * GROUP, GROUP), GROUP),
            me, tp, signal_send, signal_recv.at[group],
        )
        return carry

    lax.fori_loop(0, GROUPS, send_group, 0)

    def query(cb, carry):
        cols = pl.ds(pl.multiple_of(cb * 128, 128), 128)
        for jb in range(4):
            shortened_q[jb * 128 : jb * 128 + 128, cols] = short_conv(
                projected, halo, short_filters, 0, jb, cols
            )
        return carry

    lax.fori_loop(0, 8, query, 0)

    for load in load_tables:
        load.wait()
    cosine, sine = twist[0], twist[1]

    def forward(load_block):
        for i in range(GROUP):
            blocks = [load_block(i, jb) for jb in range(4)]
            high, low = split(
                jnp.concatenate(
                    [jnp.concatenate(blocks[:2], 1), jnp.concatenate(blocks[2:], 1)], 0
                )
            )
            turned = dot(first[...], jnp.concatenate([high, low, high], 0))
            real, imag = turned[:64], turned[64:]
            real_high, real_low = split(real * cosine + imag * sine)
            imag_high, imag_low = split(imag * cosine - real * sine)
            rows[i * 64 : i * 64 + 64, :] = jnp.concatenate(
                [real_high, imag_high, real_low, imag_low, real_high, imag_high], 1
            )
        return dot(rows[...], second[...])

    def group_rows(group):
        return pl.ds(pl.multiple_of(group * GROUP * 64, GROUP * 64), GROUP * 64)

    def filter_step(group, carry):
        spectrum[group_rows(group), :] = forward(
            lambda i, jb: filt[jb, pl.ds(group * GROUP + i, CTX, stride=OWN), :]
        )
        return carry

    wait_arrived(filt, filt_recv)
    lax.fori_loop(0, GROUPS, filter_step, 0)

    def signal_step(group, carry):
        left = forward(lambda i, jb: signal[group, jb, pl.ds(i, CTX, stride=GROUP), :])
        right = spectrum[group_rows(group), :]
        left_real, left_imag = left[:, :256], left[:, 256:]
        right_real, right_imag = right[:, :256], right[:, 256:]
        real_high, real_low = split(left_real * right_real - left_imag * right_imag)
        imag_high, imag_low = split(left_real * right_imag + left_imag * right_real)
        product = jnp.concatenate(
            [real_high, imag_high, real_low, imag_low, real_high, imag_high], 1
        )
        spectrum[group_rows(group), :] = dot(product, back_second[...])
        back(0, group)
        return carry

    def back(half, group):
        lanes = slice(128 * half, 128 * half + 128)
        imag_lanes = slice(256 + 128 * half, 384 + 128 * half)
        cosine, sine = twist[0, :, lanes], twist[1, :, lanes]
        for i in range(GROUP):
            channel = group * GROUP + i
            block = pl.ds(pl.multiple_of(channel * 64, 64), 64)
            real, imag = spectrum[block, lanes], spectrum[block, imag_lanes]
            real_high, real_low = split(real * cosine - imag * sine)
            imag_high, imag_low = split(imag * cosine + real * sine)
            result = dot(
                back_first[...],
                jnp.concatenate(
                    [real_high, imag_high, real_low, imag_low, real_high, imag_high], 0
                ),
            )
            conv[half, pl.ds(channel, CTX, stride=OWN), :] = result[:32]
            conv[half + 2, pl.ds(channel, CTX, stride=OWN), :] = result[32:]

    def back_step(group, carry):
        back(1, group)
        return carry

    def return_chunk(jb, first_row=0, count=OWN):
        chunk = pl.ds(jb, 1)

        def slab(device):
            return pl.ds(pl.multiple_of(device * OWN + first_row, GROUP), count)

        send_slabs(
            conv.at[chunk], conv_in.at[chunk], slab, slab(me),
            me, tp, conv_send.at[jb], conv_recv.at[jb],
        )

    wait_sent(filt_t, filt_send)
    def early_step(group, carry):
        wait_arrived(signal.at[group], signal_recv.at[group])
        return signal_step(group, carry)

    lax.fori_loop(0, GROUPS - 1, early_step, 0)
    return_chunk(0, 0, OWN - GROUP)
    wait_arrived(signal.at[GROUPS - 1], signal_recv.at[GROUPS - 1])
    for part in range(2):
        fetch(part).wait_recv()
    swap(2).start()
    signal_step(GROUPS - 1, 0)
    return_chunk(0, OWN - GROUP, GROUP)
    return_chunk(2)
    share(0)
    share(1)
    for load in load_weight[1:]:
        load.wait()
    for part in range(2):
        fetch(part).wait_send()

    def gather(jb, half):
        tokens = pl.ds(64 * half, 64)
        return to_tp(
            gather_out(jb).at[tokens, :], gather_in.at[jb, tokens, :],
            partner, gather_send.at[jb, half], gather_recv.at[jb, half],
        )

    def send_sum(jb, half):
        tokens = pl.ds(64 * half, 64)
        return to_tp(
            sum_out(jb).at[tokens, :], sum_in.at[jb, tokens, :],
            mate, sum_send.at[jb, half], sum_recv.at[jb, half],
        )

    def gate_chunk(jb):
        wait_arrived(conv_in.at[pl.ds(jb, 1)], conv_recv.at[jb])
        tokens = slice(jb * 128, jb * 128 + 128)
        mixed = conv_in[jb].T + skip_gain[...] * gated[tokens, :]
        gated_out[jb] = (shortened_q[tokens, :] * mixed).astype(BF16)

    def start_gather(jb):
        gather_out(jb)[...] = gated_out[jb].astype(F32)
        for half in range(2):
            gather(jb, half).start()

    def gather_sent(jb):
        for half in range(2):
            gather(jb, half).wait_send()

    def push_sums(jb):
        for half in range(2):
            tokens = slice(64 * half, 64 * half + 64)
            gather(jb, half).wait_recv()
            partner_out[tokens, :] = gather_in[jb, tokens, :].astype(BF16)
            sum_out(jb)[tokens, :] = dot(gated_out[jb, tokens, :], weight[:, columns(mate)]) + dot(
                partner_out[tokens, :], partner_weight[:, 1024:]
            )
            send_sum(jb, half).start()

    def keep_sums(jb):
        out[jb * 128 : jb * 128 + 128, :] = dot(gated_out[jb], weight[:, columns(tp)]) + dot(
            partner_out[...], partner_weight[:, :1024]
        )

    def finish(jb):
        for half in range(2):
            tokens = slice(64 * half, 64 * half + 64)
            send_sum(jb, half).wait_recv()
            out[jb * 128 + 64 * half : jb * 128 + 64 * half + 64, :] += sum_in[jb, tokens, :]

    halves = (slice(0, 512), slice(512, 1024))

    def to_far(side):
        return to_tp(
            far.at[:, halves[1 - side]], far_in.at[:, halves[1 - side]],
            (mate, partner)[side], far_send.at[side], far_recv.at[side],
        )

    def to_near(side):
        return to_tp(
            near[side], near_in[side], (mate, partner)[side], near_send.at[side], near_recv.at[side]
        )

    def relay(side):
        to_far(1 - side).wait_recv()
        near[side][:, halves[side]] += far_in[:, halves[side]]
        to_near(side).start()

    gate_chunk(0)
    far[...] = dot(gated_out[0], weight[:, columns(lax.rem(tp + 2, TP))])
    to_far(0).start()
    to_far(1).start()
    lax.fori_loop(0, GROUPS, back_step, 0)
    return_chunk(1)
    return_chunk(3)
    near[0][...] = dot(gated_out[0], weight[:, columns(mate)])
    gate_chunk(2)
    start_gather(2)
    relay(0)
    near[1][...] = dot(gated_out[0], weight[:, columns(partner)])
    out[0:128, :] = dot(gated_out[0], weight[:, columns(tp)])
    swap(2).wait_recv()
    round_quarters(0)
    for part in range(2):
        wait_arrived(shared(theirs, part), share_recv.at[part])
        swap(part).start()
    for part in range(2):
        swap(part).wait_recv()
    round_quarters(1)
    gate_chunk(1)
    gather_sent(2)
    start_gather(1)
    push_sums(2)
    keep_sums(2)
    gate_chunk(3)
    gather_sent(1)
    start_gather(3)
    push_sums(1)
    keep_sums(1)
    gather_sent(3)
    relay(1)
    push_sums(3)
    keep_sums(3)
    to_near(0).wait_recv()
    to_near(1).wait_recv()
    out[0:128, :] += near_in[0][...] + near_in[1][...]
    for jb in (2, 1, 3):
        finish(jb)
    for side in range(2):
        to_far(side).wait_send()
        to_near(side).wait_send()
    wait_sent(gated_t, signal_send)
    for part in range(2):
        wait_arrived(shared(mine, part), share_send.at[part])
        swap(part).wait_send()
    swap(2).wait_send()
    for jb in range(4):
        wait_sent(conv.at[pl.ds(jb, 1)], conv_send.at[jb])
        if jb:
            for half in range(2):
                send_sum(jb, half).wait_send()


VMEM = pl.BlockSpec(memory_space=pltpu.VMEM)
HBM = pl.BlockSpec(memory_space=pltpu.HBM)
DMA = pltpu.SemaphoreType.DMA


def per_device(projected, short_filters, long_filter, skip_gain, out_weight):
    return pl.pallas_call(
        mixer_kernel,
        out_shape=jax.ShapeDtypeStruct((512, 1024), F32),
        in_specs=[HBM, VMEM, HBM, VMEM, HBM] + [HBM] * 5,
        out_specs=VMEM,
        scratch_shapes=[
            pltpu.VMEM((3, 512, 1024), F32),
            pltpu.VMEM((512, 1024), F32),
            pltpu.VMEM((1024, 4096), BF16),
            pltpu.VMEM((128, 192), BF16),
            pltpu.VMEM((2, 64, 256), F32),
            pltpu.VMEM((1536, 512), BF16),
            pltpu.VMEM((1536, 512), BF16),
            pltpu.VMEM((64, 384), BF16),
            pltpu.VMEM((3, 8, 1024), F32),
            pltpu.VMEM((3, 8, 1024), F32),
            pltpu.VMEM((4, 1024, 128), F32),
            pltpu.VMEM((4, 1024, 128), F32),
            pltpu.VMEM((4, 1024, 128), F32),
            pltpu.VMEM((GROUPS, 4, CTX * GROUP, 128), F32),
            pltpu.VMEM((512, 1024), F32),
            pltpu.VMEM((GROUP * 64, 1536), BF16),
            pltpu.VMEM((OWN * 64, 512), F32),
            pltpu.VMEM((4, 1024, 128), F32),
            pltpu.VMEM((4, 128, 1024), BF16),
            pltpu.VMEM((128, 1024), BF16),
            pltpu.VMEM((1024, 2048), F32),
            pltpu.VMEM((1024, 2048), BF16),
            pltpu.VMEM((4, 128, 1024), F32),
            pltpu.VMEM((4, 128, 1024), F32),
            pltpu.VMEM((128, 1024), F32),
            DMA((12,)),
            DMA,
            DMA,
            DMA,
            DMA,
            DMA,
            DMA((GROUPS,)),
            DMA((4,)),
            DMA((4,)),
            DMA((2,)),
            DMA((2,)),
            DMA((2,)),
            DMA((2,)),
            DMA((3,)),
            DMA((3,)),
            DMA((4, 2)),
            DMA((4, 2)),
            DMA((4, 2)),
            DMA((4, 2)),
            DMA((2,)),
            DMA((2,)),
            DMA((2,)),
            DMA((2,)),
        ],
        compiler_params=pltpu.CompilerParams(
            collective_id=0, has_side_effects=True, vmem_limit_bytes=60 * 2**20
        ),
        name="mixer",
    )(
        projected, short_filters, long_filter, skip_gain[None], out_weight,
        *[jnp.asarray(table) for table in tables()],
    )


def solution(mesh):
    return jax.shard_map(
        per_device,
        mesh=mesh,
        in_specs=(
            P(None, "ctx", "tp"),
            P(None, None, "tp"),
            P("ctx", "tp"),
            P("tp"),
            P("tp", None),
        ),
        out_specs=P("ctx", "tp"),
        check_vma=False,
    )
```

```python
import jax
import jax.numpy as jnp
import ml_dtypes
import numpy as np
from jax import lax
from jax.experimental import pallas as pl
from jax.experimental.pallas import tpu as pltpu
from jax.sharding import PartitionSpec as P

MESH = pl.DeviceIdType.MESH
BF16 = jnp.bfloat16
F32 = jnp.float32
CTX = 32
TP = 4
OWN = 32
GROUP = 8
GROUPS = OWN // GROUP
CHIP_OFFSETS = (
    (1, 0), (3, 0), (0, 1), (0, 3), (1, 1), (3, 3), (1, 3), (3, 1),
    (2, 0), (0, 2), (2, 1), (2, 3), (1, 2), (3, 2), (2, 2),
)
PEERS = tuple((a, b, d) for a, b in CHIP_OFFSETS for d in (0, 1)) + ((0, 0, 1),)


def split_np(table):
    high = table.astype(ml_dtypes.bfloat16)
    low = (table - high.astype(np.float64)).astype(ml_dtypes.bfloat16)
    return high, low


def tables():
    block = np.arange(32)
    n1 = np.concatenate([2 * block, 2 * block + 1]).astype(np.float64)
    k1 = np.arange(64) + 0.25
    n2 = np.arange(256)
    psi = 2 * np.pi * np.outer(k1, n1) / 64
    high, low = split_np(np.concatenate([np.cos(psi), -np.sin(psi)], 0))
    first = np.concatenate([high, high, low], 1)
    phi = 2 * np.pi * np.outer(k1, n2) / 16384
    twist = np.stack([np.cos(phi), np.sin(phi)]).astype(np.float32)
    theta = 2 * np.pi * (np.outer(n2, n2) % 256) / 256
    cosine, sine = np.cos(theta), np.sin(theta)
    high, low = split_np(np.block([[cosine, -sine], [sine, cosine]]))
    second = np.concatenate([high, high, low], 0)
    high, low = split_np(np.block([[cosine, sine], [-sine, cosine]]))
    back_second = np.concatenate([high, high, low], 0)
    high, low = split_np(np.concatenate([np.cos(psi.T), -np.sin(psi.T)], 1) / 16384)
    back_first = np.concatenate([high, high, low], 1)
    return first, twist, second, back_second, back_first


def split(value):
    high = value.astype(BF16)
    return high, (value - high.astype(F32)).astype(BF16)


def dot(left, right):
    return jnp.dot(left, right, preferred_element_type=F32)


def ctx_peer(me, offset):
    a, b, d = offset
    return (me // 8 + a) % 4 * 8 + (me // 2 + b) % 4 * 2 + (me + d) % 2


def rows_of(device):
    return pl.ds(pl.multiple_of(device * OWN, OWN), OWN)


def send_slabs(source, target, slab, own_slab, me, tp, send_sem, recv_sem):
    pltpu.make_async_copy(
        source.at[:, slab(me), :], target.at[:, own_slab, :], recv_sem
    ).start()
    for offset in PEERS:
        peer = ctx_peer(me, offset)
        pltpu.make_async_remote_copy(
            src_ref=source.at[:, slab(peer), :],
            dst_ref=target.at[:, own_slab, :],
            send_sem=send_sem,
            recv_sem=recv_sem,
            device_id=(peer, tp),
            device_id_type=MESH,
        ).start()


def wait_arrived(target, recv_sem):
    pltpu.make_async_copy(target, target, recv_sem).wait()


def wait_sent(source, send_sem):
    away = source.at[:, 0 : (CTX - 1) * OWN, :]
    pltpu.make_async_copy(away, away, send_sem).wait()


def short_conv(projected, halo, short_filters, stream, jb, cols):
    rows = projected[stream, jb * 128 : jb * 128 + 128, cols]
    before = halo[stream, :, cols] if jb == 0 else projected[stream, jb * 128 - 8 : jb * 128, cols]
    longer = jnp.concatenate([before, rows], 0)
    taps = short_filters[stream, :, cols]
    return taps[0:1] * rows + taps[1:2] * longer[7:135] + taps[2:3] * longer[6:134]


def mixer_kernel(
    projected_hbm, short_filters, long_filter_hbm, skip_gain, weight_hbm,
    first_hbm, twist_hbm, second_hbm, back_second_hbm, back_first_hbm,
    kept_hbm, sum_in, near_in_partner,
    kept,
    projected, long_filter, weight, first, twist, second, back_second, back_first,
    halo, halo_in, filt_t, gated_t, filt, signal,
    shortened_q, rows, spectrum, conv_in, gated_out, partner_out, weight_in, partner_weight,
    gather_in,
    load_sem, halo_send, halo_recv, filt_send, filt_recv, signal_send, signal_recv,
    conv_send, conv_recv, fetch_send, fetch_recv, share_send, share_recv, swap_send, swap_recv,
    gather_send, gather_recv, sum_send, sum_recv, far_send, far_recv, near_send, near_recv, kept_sem,
):
    me = lax.axis_index("ctx")
    tp = lax.axis_index("tp")
    partner, mate = tp + 1 - 2 * (tp % 2), TP - 1 - tp
    parity = (me // 8 + me // 2) % 2
    mine, theirs = 2 * parity + me % 2, 2 * (1 - parity) + me % 2
    conv = filt_t
    gated = long_filter
    fetch_out = kept

    def sum_out(jb):
        return projected.at[0, pl.ds(jb * 128, 128), :]

    def gather_out(jb):
        return projected.at[1, pl.ds(jb * 128, 128), :]

    far = projected.at[0, pl.ds(0, 128), :]
    near = (projected.at[1, pl.ds(0, 128), :], projected.at[2, pl.ds(0, 128), :])
    far_in, near_in = gather_in.at[0], (sum_in.at[0], near_in_partner)

    def columns(quarter):
        return pl.ds(pl.multiple_of(quarter * 1024, 1024), 1024)

    def quarter_rows(quarter):
        return pl.ds(pl.multiple_of(quarter * 256, 256), 256)

    def to_tp(source, target, device, send_sem, recv_sem):
        return pltpu.make_async_remote_copy(
            src_ref=source,
            dst_ref=target,
            send_sem=send_sem,
            recv_sem=recv_sem,
            device_id=(me, device),
            device_id_type=MESH,
        )

    def fetch(part):
        return to_tp(
            fetch_out.at[pl.ds(part * 256, 256), :],
            weight_in.at[quarter_rows(mine), pl.ds(part * 1024, 1024)],
            partner, fetch_send.at[part], fetch_recv.at[part],
        )

    def fetch_rest(part):
        rest = pl.ds(pl.multiple_of(theirs * 256 + 192, 64), 64)
        return to_tp(
            projected.at[2, pl.ds(part * 64, 64), :],
            weight_in.at[rest, pl.ds(part * 1024, 1024)],
            partner, fetch_send.at[2 + part], fetch_recv.at[2 + part],
        )

    def share(part):
        for direction, offset in enumerate(((1, 0, 0), (3, 0, 0), (0, 1, 0), (0, 3, 0))):
            first_row = mine * 256 + (128 + direction * 16 if part else direction * 32)
            slab = weight_in.at[pl.ds(pl.multiple_of(first_row, 16), 16 if part else 32), :]
            pltpu.make_async_remote_copy(
                src_ref=slab,
                dst_ref=slab,
                send_sem=share_send.at[part],
                recv_sem=share_recv.at[part],
                device_id=(ctx_peer(me, offset), tp),
                device_id_type=MESH,
            ).start()

    def shared(quarter, part):
        first_row, count = ((0, 128), (128, 64), (192, 64))[part]
        return weight_in.at[pl.ds(pl.multiple_of(quarter * 256 + first_row, 64), count), :]

    def swap(which):
        slab = weight_in.at[quarter_rows(mine), :] if which == 3 else shared(theirs, which)
        return pltpu.make_async_remote_copy(
            src_ref=slab,
            dst_ref=slab,
            send_sem=swap_send.at[which],
            recv_sem=swap_recv.at[which],
            device_id=(ctx_peer(me, (0, 0, 1)), tp),
            device_id_type=MESH,
        )

    def round_quarters(which):
        first_row = ((parity, 1 - parity)[which]) * 512

        def step(i, carry):
            block = pl.ds(pl.multiple_of(first_row + i * 64, 64), 64)
            partner_weight[block, :] = weight_in[block, :].astype(BF16)
            return carry

        lax.fori_loop(0, 8, step, 0)

    barrier = pltpu.get_barrier_semaphore()

    def signal_peer(i, carry):
        pl.semaphore_signal(
            barrier, inc=1, device_id=(lax.rem(me + i, CTX), tp), device_id_type=MESH
        )
        return carry

    lax.fori_loop(1, CTX, signal_peer, 0)
    for side in (partner, mate):
        pl.semaphore_signal(barrier, inc=1, device_id=(me, side), device_id_type=MESH)
    load_filter = pltpu.make_async_copy(long_filter_hbm, long_filter, load_sem.at[0])
    load_filter.start()
    load_projected = pltpu.make_async_copy(projected_hbm, projected, load_sem.at[1])
    load_projected.start()
    load_weight = [
        pltpu.make_async_copy(
            weight_hbm.at[quarter_rows(lax.rem(mine + i, 4)), :],
            weight.at[quarter_rows(lax.rem(mine + i, 4)), :],
            load_sem.at[8 + i],
        )
        for i in range(4)
    ]
    load_weight[0].start()
    load_filter.wait()

    def turn_filter(cb, carry):
        cols = pl.ds(pl.multiple_of(cb * 128, 128), 128)
        for jb in range(4):
            filt_t[jb, cols, :] = long_filter[jb * 128 : jb * 128 + 128, cols].T
        return carry

    lax.fori_loop(0, 8, turn_filter, 0)
    load_weight[0].wait()
    for part, quarter in enumerate((partner, TP - 1 - partner)):
        fetch_out[part * 256 : part * 256 + 256, :] = weight[
            quarter_rows(mine), columns(quarter)
        ].astype(F32)
    pl.semaphore_wait(barrier, CTX + 1)

    edge = pltpu.make_async_remote_copy(
        src_ref=projected_hbm.at[:, 504:512, :],
        dst_ref=halo_in,
        send_sem=halo_send,
        recv_sem=halo_recv,
        device_id=(lax.rem(me + 1, CTX), tp),
        device_id_type=MESH,
    )
    edge.start()
    for half in range(2):
        part = pl.ds(2 * half, 2)
        send_slabs(
            filt_t.at[part], filt.at[part], rows_of, rows_of(me), me, tp, filt_send, filt_recv
        )
    fetch(0).start()
    fetch(1).start()
    load_projected.wait()
    load_tables = [
        pltpu.make_async_copy(source, target, load_sem.at[3 + i])
        for i, (source, target) in enumerate(
            (
                (first_hbm, first), (twist_hbm, twist), (second_hbm, second),
                (back_second_hbm, back_second), (back_first_hbm, back_first),
            )
        )
    ]
    for load in load_tables:
        load.start()
    for load in load_weight[1:]:
        load.start()
    edge.wait()
    halo[...] = jnp.where(me > 0, halo_in[...], 0.0)

    def gate(cb, carry):
        cols = pl.ds(pl.multiple_of(cb * 128, 128), 128)
        for jb in range(4):
            key = short_conv(projected, halo, short_filters, 1, jb, cols)
            value = short_conv(projected, halo, short_filters, 2, jb, cols)
            product = key * value
            gated[jb * 128 : jb * 128 + 128, cols] = product
            gated_t[jb, cols, :] = product.T
        return carry

    lax.fori_loop(0, 8, gate, 0)

    def send_group(group, carry):
        def slab(device):
            return pl.ds(pl.multiple_of(device * OWN + group * GROUP, GROUP), GROUP)

        send_slabs(
            gated_t, signal.at[group], slab, pl.ds(pl.multiple_of(me * GROUP, GROUP), GROUP),
            me, tp, signal_send, signal_recv.at[group],
        )
        return carry

    lax.fori_loop(0, GROUPS, send_group, 0)

    def query(cb, carry):
        cols = pl.ds(pl.multiple_of(cb * 128, 128), 128)
        for jb in range(4):
            shortened_q[jb * 128 : jb * 128 + 128, cols] = short_conv(
                projected, halo, short_filters, 0, jb, cols
            )
        return carry

    lax.fori_loop(0, 8, query, 0)

    load_weight[2].wait()
    for part, quarter in enumerate((partner, TP - 1 - partner)):
        rest = pl.ds(pl.multiple_of(theirs * 256 + 192, 64), 64)
        projected[2, part * 64 : part * 64 + 64, :] = weight[rest, columns(quarter)].astype(F32)
        fetch_rest(part).start()

    for load in load_tables:
        load.wait()
    cosine, sine = twist[0], twist[1]

    def forward(load_block):
        for i in range(GROUP):
            blocks = [load_block(i, jb) for jb in range(4)]
            high, low = split(
                jnp.concatenate(
                    [jnp.concatenate(blocks[:2], 1), jnp.concatenate(blocks[2:], 1)], 0
                )
            )
            turned = dot(first[...], jnp.concatenate([high, low, high], 0))
            real, imag = turned[:64], turned[64:]
            real_high, real_low = split(real * cosine + imag * sine)
            imag_high, imag_low = split(imag * cosine - real * sine)
            rows[i * 64 : i * 64 + 64, :] = jnp.concatenate(
                [real_high, imag_high, real_low, imag_low, real_high, imag_high], 1
            )
        return dot(rows[...], second[...])

    def group_rows(group):
        return pl.ds(pl.multiple_of(group * GROUP * 64, GROUP * 64), GROUP * 64)

    def filter_step(group, carry):
        spectrum[group_rows(group), :] = forward(
            lambda i, jb: filt[jb, pl.ds(group * GROUP + i, CTX, stride=OWN), :]
        )
        return carry

    wait_arrived(filt, filt_recv)
    lax.fori_loop(0, GROUPS, filter_step, 0)

    def signal_step(group, carry):
        left = forward(lambda i, jb: signal[group, jb, pl.ds(i, CTX, stride=GROUP), :])
        right = spectrum[group_rows(group), :]
        left_real, left_imag = left[:, :256], left[:, 256:]
        right_real, right_imag = right[:, :256], right[:, 256:]
        real_high, real_low = split(left_real * right_real - left_imag * right_imag)
        imag_high, imag_low = split(left_real * right_imag + left_imag * right_real)
        product = jnp.concatenate(
            [real_high, imag_high, real_low, imag_low, real_high, imag_high], 1
        )
        spectrum[group_rows(group), :] = dot(product, back_second[...])
        back(0, group)
        return carry

    def back(half, group):
        lanes = slice(128 * half, 128 * half + 128)
        imag_lanes = slice(256 + 128 * half, 384 + 128 * half)
        cosine, sine = twist[0, :, lanes], twist[1, :, lanes]
        for i in range(GROUP):
            channel = group * GROUP + i
            block = pl.ds(pl.multiple_of(channel * 64, 64), 64)
            real, imag = spectrum[block, lanes], spectrum[block, imag_lanes]
            real_high, real_low = split(real * cosine - imag * sine)
            imag_high, imag_low = split(imag * cosine + real * sine)
            result = dot(
                back_first[...],
                jnp.concatenate(
                    [real_high, imag_high, real_low, imag_low, real_high, imag_high], 0
                ),
            )
            conv[half, pl.ds(channel, CTX, stride=OWN), :] = result[:32]
            conv[half + 2, pl.ds(channel, CTX, stride=OWN), :] = result[32:]

    def back_step(group, carry):
        back(1, group)
        return carry

    def return_chunk(jb, first_row=0, count=OWN):
        chunk = pl.ds(jb, 1)

        def slab(device):
            return pl.ds(pl.multiple_of(device * OWN + first_row, GROUP), count)

        send_slabs(
            conv.at[chunk], conv_in.at[chunk], slab, slab(me),
            me, tp, conv_send.at[jb], conv_recv.at[jb],
        )

    wait_sent(filt_t, filt_send)
    def early_step(group, carry):
        wait_arrived(signal.at[group], signal_recv.at[group])
        return signal_step(group, carry)

    lax.fori_loop(0, GROUPS - 1, early_step, 0)
    return_chunk(0, 0, OWN - GROUP)
    wait_arrived(signal.at[GROUPS - 1], signal_recv.at[GROUPS - 1])
    for part in range(2):
        fetch(part).wait_recv()
    swap(3).start()
    signal_step(GROUPS - 1, 0)
    return_chunk(0, OWN - GROUP, GROUP)
    return_chunk(2)
    share(0)
    share(1)
    load_weight[1].wait()
    load_weight[3].wait()
    for part in range(2):
        fetch(part).wait_send()
        fetch_rest(part).wait_send()
        fetch_rest(part).wait_recv()
    swap(2).start()

    def gather(jb, half):
        tokens = pl.ds(64 * half, 64)
        return to_tp(
            gather_out(jb).at[tokens, :], gather_in.at[jb, tokens, :],
            partner, gather_send.at[jb, half], gather_recv.at[jb, half],
        )

    def send_sum(jb, half):
        tokens = pl.ds(64 * half, 64)
        return to_tp(
            sum_out(jb).at[tokens, :], sum_in.at[jb, tokens, :],
            mate, sum_send.at[jb, half], sum_recv.at[jb, half],
        )

    def gate_chunk(jb):
        wait_arrived(conv_in.at[pl.ds(jb, 1)], conv_recv.at[jb])
        tokens = slice(jb * 128, jb * 128 + 128)
        mixed = conv_in[jb].T + skip_gain[...] * gated[tokens, :]
        gated_out[jb] = (shortened_q[tokens, :] * mixed).astype(BF16)

    def start_gather(jb):
        gather_out(jb)[...] = gated_out[jb].astype(F32)
        for half in range(2):
            gather(jb, half).start()

    def gather_sent(jb):
        for half in range(2):
            gather(jb, half).wait_send()

    def push_sums(jb):
        for half in range(2):
            tokens = slice(64 * half, 64 * half + 64)
            gather(jb, half).wait_recv()
            partner_out[tokens, :] = gather_in[jb, tokens, :].astype(BF16)
            sum_out(jb)[tokens, :] = dot(gated_out[jb, tokens, :], weight[:, columns(mate)]) + dot(
                partner_out[tokens, :], partner_weight[:, 1024:]
            )
            send_sum(jb, half).start()

    def keep_sums(jb):
        kept[jb * 128 : jb * 128 + 128, :] = dot(gated_out[jb], weight[:, columns(tp)]) + dot(
            partner_out[...], partner_weight[:, :1024]
        )
        store(jb).start()

    def store(jb):
        tokens = pl.ds(jb * 128, 128)
        return pltpu.make_async_copy(
            kept.at[tokens, :], kept_hbm.at[tokens, :], kept_sem.at[jb]
        )

    halves = (slice(0, 512), slice(512, 1024))

    def to_far(side):
        return to_tp(
            far.at[:, halves[1 - side]], far_in.at[:, halves[1 - side]],
            (mate, partner)[side], far_send.at[side], far_recv.at[side],
        )

    def to_near(side, part):
        half = halves[side] if part else halves[1 - side]
        return to_tp(
            near[side].at[:, half], near_in[side].at[:, half],
            (mate, partner)[side], near_send.at[side, part], near_recv.at[side, part],
        )

    def relay(side):
        to_far(1 - side).wait_recv()
        near[side][:, halves[side]] += far_in[:, halves[side]]
        to_near(side, 1).start()

    gate_chunk(0)
    for side in range(2):
        first_column = lax.rem(tp + 2, TP) * 1024 + 512 * (1 - side)
        far[:, halves[1 - side]] = dot(
            gated_out[0], weight[:, pl.ds(pl.multiple_of(first_column, 512), 512)]
        )
        to_far(side).start()
    near[0][...] = dot(gated_out[0], weight[:, columns(mate)])
    to_near(0, 0).start()
    lax.fori_loop(0, GROUPS, back_step, 0)
    return_chunk(1)
    return_chunk(3)
    gate_chunk(2)
    start_gather(2)
    relay(0)
    near[1][...] = dot(gated_out[0], weight[:, columns(partner)])
    kept[0:128, :] = dot(gated_out[0], weight[:, columns(tp)])
    store(0).start()
    swap(3).wait_recv()
    round_quarters(0)
    for part in range(2):
        wait_arrived(shared(theirs, part), share_recv.at[part])
        swap(part).start()
    for part in range(3):
        swap(part).wait_recv()
    round_quarters(1)
    gate_chunk(1)
    gather_sent(2)
    start_gather(1)
    push_sums(2)
    keep_sums(2)
    gate_chunk(3)
    gather_sent(1)
    start_gather(3)
    push_sums(1)
    keep_sums(1)
    gather_sent(3)
    to_near(1, 0).start()
    relay(1)
    push_sums(3)
    keep_sums(3)
    for side in range(2):
        to_far(side).wait_send()
        for part in range(2):
            to_near(side, part).wait()
    for jb in range(4):
        store(jb).wait()
        if jb:
            for half in range(2):
                send_sum(jb, half).wait()
    wait_sent(gated_t, signal_send)
    for part in range(2):
        wait_arrived(shared(mine, part), share_send.at[part])
        swap(part).wait_send()
    swap(2).wait_send()
    swap(3).wait_send()
    for jb in range(4):
        wait_sent(conv.at[pl.ds(jb, 1)], conv_send.at[jb])


def add_kernel(kept, landed, landed_chunk, total, left, right, first_chunk, load_sem, store_sem):
    chunks = [pl.ds(128 * jb, 128) for jb in range(4)]
    loads = [pltpu.make_async_copy(landed_chunk, first_chunk, load_sem.at[8])]
    for jb, chunk in enumerate(chunks):
        loads.append(pltpu.make_async_copy(kept.at[chunk, :], left.at[chunk, :], load_sem.at[jb]))
        loads.append(
            pltpu.make_async_copy(landed.at[chunk, :], right.at[chunk, :], load_sem.at[4 + jb])
        )
    for load in loads:
        load.start()
    loads[0].wait()
    stores = []
    for jb, chunk in enumerate(chunks):
        loads[1 + 2 * jb].wait()
        loads[2 + 2 * jb].wait()
        value = left[chunk, :] + right[chunk, :]
        left[chunk, :] = value + first_chunk[...] if jb == 0 else value
        stores.append(
            pltpu.make_async_copy(left.at[chunk, :], total.at[chunk, :], store_sem.at[jb])
        )
        stores[jb].start()
    for store in stores:
        store.wait()


VMEM = pl.BlockSpec(memory_space=pltpu.VMEM)
HBM = pl.BlockSpec(memory_space=pltpu.HBM)
DMA = pltpu.SemaphoreType.DMA


def per_device(projected, short_filters, long_filter, skip_gain, out_weight):
    kept, landed, landed_chunk = pl.pallas_call(
        mixer_kernel,
        out_shape=(
            jax.ShapeDtypeStruct((512, 1024), F32),
            jax.ShapeDtypeStruct((4, 128, 1024), F32),
            jax.ShapeDtypeStruct((128, 1024), F32),
        ),
        in_specs=[HBM, VMEM, HBM, VMEM, HBM] + [HBM] * 5,
        out_specs=(HBM, HBM, HBM),
        scratch_shapes=[
            pltpu.VMEM((512, 1024), F32),
            pltpu.VMEM((3, 512, 1024), F32),
            pltpu.VMEM((512, 1024), F32),
            pltpu.VMEM((1024, 4096), BF16),
            pltpu.VMEM((128, 192), BF16),
            pltpu.VMEM((2, 64, 256), F32),
            pltpu.VMEM((1536, 512), BF16),
            pltpu.VMEM((1536, 512), BF16),
            pltpu.VMEM((64, 384), BF16),
            pltpu.VMEM((3, 8, 1024), F32),
            pltpu.VMEM((3, 8, 1024), F32),
            pltpu.VMEM((4, 1024, 128), F32),
            pltpu.VMEM((4, 1024, 128), F32),
            pltpu.VMEM((4, 1024, 128), F32),
            pltpu.VMEM((GROUPS, 4, CTX * GROUP, 128), F32),
            pltpu.VMEM((512, 1024), F32),
            pltpu.VMEM((GROUP * 64, 1536), BF16),
            pltpu.VMEM((OWN * 64, 512), F32),
            pltpu.VMEM((4, 1024, 128), F32),
            pltpu.VMEM((4, 128, 1024), BF16),
            pltpu.VMEM((128, 1024), BF16),
            pltpu.VMEM((1024, 2048), F32),
            pltpu.VMEM((1024, 2048), BF16),
            pltpu.VMEM((4, 128, 1024), F32),
            DMA((12,)),
            DMA,
            DMA,
            DMA,
            DMA,
            DMA,
            DMA((GROUPS,)),
            DMA((4,)),
            DMA((4,)),
            DMA((4,)),
            DMA((4,)),
            DMA((2,)),
            DMA((2,)),
            DMA((4,)),
            DMA((4,)),
            DMA((4, 2)),
            DMA((4, 2)),
            DMA((4, 2)),
            DMA((4, 2)),
            DMA((2,)),
            DMA((2,)),
            DMA((2, 2)),
            DMA((2, 2)),
            DMA((4,)),
        ],
        compiler_params=pltpu.CompilerParams(
            collective_id=0, has_side_effects=True, vmem_limit_bytes=60 * 2**20
        ),
        name="mixer",
    )(
        projected, short_filters, long_filter, skip_gain[None], out_weight,
        *[jnp.asarray(table) for table in tables()],
    )
    return pl.pallas_call(
        add_kernel,
        out_shape=jax.ShapeDtypeStruct((512, 1024), F32),
        in_specs=[HBM] * 3,
        out_specs=HBM,
        scratch_shapes=[
            pltpu.VMEM((512, 1024), F32),
            pltpu.VMEM((512, 1024), F32),
            pltpu.VMEM((128, 1024), F32),
            DMA((9,)),
            DMA((4,)),
        ],
        compiler_params=pltpu.CompilerParams(vmem_limit_bytes=60 * 2**20),
        name="add",
    )(kept, landed.reshape(512, 1024), landed_chunk)


def solution(mesh):
    return jax.shard_map(
        per_device,
        mesh=mesh,
        in_specs=(
            P(None, "ctx", "tp"),
            P(None, None, "tp"),
            P("ctx", "tp"),
            P("tp"),
            P("tp", None),
        ),
        out_specs=P("ctx", "tp"),
        check_vma=False,
    )
```

```python
import jax
import jax.numpy as jnp
import ml_dtypes
import numpy as np
from jax import lax
from jax.experimental import pallas as pl
from jax.experimental.pallas import tpu as pltpu
from jax.sharding import PartitionSpec as P

MESH = pl.DeviceIdType.MESH
BF16 = jnp.bfloat16
F32 = jnp.float32
CTX = 32
TP = 4
OWN = 32
GROUP = 8
GROUPS = OWN // GROUP
CHIP_OFFSETS = (
    (1, 0), (3, 0), (0, 1), (0, 3), (1, 1), (3, 3), (1, 3), (3, 1),
    (2, 0), (0, 2), (2, 1), (2, 3), (1, 2), (3, 2), (2, 2),
)
PEERS = tuple((a, b, d) for a, b in CHIP_OFFSETS for d in (0, 1)) + ((0, 0, 1),)


def split_np(table):
    high = table.astype(ml_dtypes.bfloat16)
    low = (table - high.astype(np.float64)).astype(ml_dtypes.bfloat16)
    return high, low


def tables():
    block = np.arange(32)
    n1 = np.concatenate([2 * block, 2 * block + 1]).astype(np.float64)
    k1 = np.arange(64) + 0.25
    n2 = np.arange(256)
    psi = 2 * np.pi * np.outer(k1, n1) / 64
    high, low = split_np(np.concatenate([np.cos(psi), -np.sin(psi)], 0))
    first = np.concatenate([high, high, low], 1)
    phi = 2 * np.pi * np.outer(k1, n2) / 16384
    twist = np.stack([np.cos(phi), np.sin(phi)]).astype(np.float32)
    theta = 2 * np.pi * (np.outer(n2, n2) % 256) / 256
    cosine, sine = np.cos(theta), np.sin(theta)
    high, low = split_np(np.block([[cosine, -sine], [sine, cosine]]))
    second = np.concatenate([high, high, low], 0)
    high, low = split_np(np.block([[cosine, sine], [-sine, cosine]]))
    back_second = np.concatenate([high, high, low], 0)
    high, low = split_np(np.concatenate([np.cos(psi.T), -np.sin(psi.T)], 1) / 16384)
    back_first = np.concatenate([high, high, low], 1)
    return first, twist, second, back_second, back_first


def split(value):
    high = value.astype(BF16)
    return high, (value - high.astype(F32)).astype(BF16)


def dot(left, right):
    return jnp.dot(left, right, preferred_element_type=F32)


def ctx_peer(me, offset):
    a, b, d = offset
    return (me // 8 + a) % 4 * 8 + (me // 2 + b) % 4 * 2 + (me + d) % 2


def rows_of(device):
    return pl.ds(pl.multiple_of(device * OWN, OWN), OWN)


def send_slabs(source, target, slab, own_slab, me, tp, send_sem, recv_sem):
    pltpu.make_async_copy(
        source.at[:, slab(me), :], target.at[:, own_slab, :], recv_sem
    ).start()
    for offset in PEERS:
        peer = ctx_peer(me, offset)
        pltpu.make_async_remote_copy(
            src_ref=source.at[:, slab(peer), :],
            dst_ref=target.at[:, own_slab, :],
            send_sem=send_sem,
            recv_sem=recv_sem,
            device_id=(peer, tp),
            device_id_type=MESH,
        ).start()


def wait_arrived(target, recv_sem):
    pltpu.make_async_copy(target, target, recv_sem).wait()


def wait_sent(source, send_sem):
    away = source.at[:, 0 : (CTX - 1) * OWN, :]
    pltpu.make_async_copy(away, away, send_sem).wait()


def short_conv(projected, halo, short_filters, stream, jb, cols):
    rows = projected[stream, jb * 128 : jb * 128 + 128, cols]
    before = halo[stream, :, cols] if jb == 0 else projected[stream, jb * 128 - 8 : jb * 128, cols]
    longer = jnp.concatenate([before, rows], 0)
    taps = short_filters[stream, :, cols]
    return taps[0:1] * rows + taps[1:2] * longer[7:135] + taps[2:3] * longer[6:134]


def mixer_kernel(
    projected_hbm, short_filters, long_filter_hbm, skip_gain, weight_hbm,
    first_hbm, twist_hbm, second_hbm, back_second_hbm, back_first_hbm,
    kept_hbm, sum_in, near_in_partner,
    kept,
    projected, long_filter, weight, first, twist, second, back_second, back_first,
    halo, halo_in, filt_t, gated_t, filt, signal,
    shortened_q, rows, spectrum, conv_in, gated_out, partner_out, weight_in, partner_weight,
    gather_in,
    load_sem, halo_send, halo_recv, filt_send, filt_recv, signal_send, signal_recv,
    conv_send, conv_recv, fetch_send, fetch_recv, share_send, share_recv, swap_send, swap_recv,
    gather_send, gather_recv, sum_send, sum_recv, far_send, far_recv, near_send, near_recv, kept_sem,
):
    me = lax.axis_index("ctx")
    tp = lax.axis_index("tp")
    partner, mate = tp + 1 - 2 * (tp % 2), TP - 1 - tp
    parity = (me // 8 + me // 2) % 2
    mine, theirs = 2 * parity + me % 2, 2 * (1 - parity) + me % 2
    conv = filt_t
    gated = long_filter
    fetch_out = kept

    def sum_out(jb):
        return projected.at[0, pl.ds(jb * 128, 128), :]

    def gather_out(jb):
        return projected.at[1, pl.ds(jb * 128, 128), :]

    far = projected.at[0, pl.ds(0, 128), :]
    near = (projected.at[1, pl.ds(0, 128), :], projected.at[2, pl.ds(0, 128), :])
    far_in, near_in = gather_in.at[0], (sum_in.at[0], near_in_partner)

    def columns(quarter):
        return pl.ds(pl.multiple_of(quarter * 1024, 1024), 1024)

    def quarter_rows(quarter):
        return pl.ds(pl.multiple_of(quarter * 256, 256), 256)

    def to_tp(source, target, device, send_sem, recv_sem):
        return pltpu.make_async_remote_copy(
            src_ref=source,
            dst_ref=target,
            send_sem=send_sem,
            recv_sem=recv_sem,
            device_id=(me, device),
            device_id_type=MESH,
        )

    def fetch(part):
        return to_tp(
            fetch_out.at[pl.ds(part * 256, 256), :],
            weight_in.at[quarter_rows(mine), pl.ds(part * 1024, 1024)],
            partner, fetch_send.at[part], fetch_recv.at[part],
        )

    def fetch_rest(part):
        rest = pl.ds(pl.multiple_of(theirs * 256 + 192, 64), 64)
        return to_tp(
            projected.at[2, pl.ds(part * 64, 64), :],
            weight_in.at[rest, pl.ds(part * 1024, 1024)],
            partner, fetch_send.at[2 + part], fetch_recv.at[2 + part],
        )

    def share(part):
        for direction, offset in enumerate(((1, 0, 0), (3, 0, 0), (0, 1, 0), (0, 3, 0))):
            first_row = mine * 256 + (128 + direction * 16 if part else direction * 32)
            slab = weight_in.at[pl.ds(pl.multiple_of(first_row, 16), 16 if part else 32), :]
            pltpu.make_async_remote_copy(
                src_ref=slab,
                dst_ref=slab,
                send_sem=share_send.at[part],
                recv_sem=share_recv.at[part],
                device_id=(ctx_peer(me, offset), tp),
                device_id_type=MESH,
            ).start()

    def shared(quarter, part):
        first_row, count = ((0, 128), (128, 64), (192, 64))[part]
        return weight_in.at[pl.ds(pl.multiple_of(quarter * 256 + first_row, 64), count), :]

    def swap(which):
        slab = weight_in.at[quarter_rows(mine), :] if which == 3 else shared(theirs, which)
        return pltpu.make_async_remote_copy(
            src_ref=slab,
            dst_ref=slab,
            send_sem=swap_send.at[which],
            recv_sem=swap_recv.at[which],
            device_id=(ctx_peer(me, (0, 0, 1)), tp),
            device_id_type=MESH,
        )

    def round_quarters(which):
        first_row = ((parity, 1 - parity)[which]) * 512

        def step(i, carry):
            block = pl.ds(pl.multiple_of(first_row + i * 64, 64), 64)
            partner_weight[block, :] = weight_in[block, :].astype(BF16)
            return carry

        lax.fori_loop(0, 8, step, 0)

    barrier = pltpu.get_barrier_semaphore()

    def signal_peer(i, carry):
        pl.semaphore_signal(
            barrier, inc=1, device_id=(lax.rem(me + i, CTX), tp), device_id_type=MESH
        )
        return carry

    lax.fori_loop(1, CTX, signal_peer, 0)
    for side in (partner, mate):
        pl.semaphore_signal(barrier, inc=1, device_id=(me, side), device_id_type=MESH)
    load_filter = pltpu.make_async_copy(long_filter_hbm, long_filter, load_sem.at[0])
    load_filter.start()
    load_projected = pltpu.make_async_copy(projected_hbm, projected, load_sem.at[1])
    load_projected.start()
    load_weight = [
        pltpu.make_async_copy(
            weight_hbm.at[quarter_rows(lax.rem(mine + i, 4)), :],
            weight.at[quarter_rows(lax.rem(mine + i, 4)), :],
            load_sem.at[8 + i],
        )
        for i in range(4)
    ]
    load_weight[0].start()
    load_filter.wait()

    def turn_filter(cb, carry):
        cols = pl.ds(pl.multiple_of(cb * 128, 128), 128)
        for jb in range(4):
            filt_t[jb, cols, :] = long_filter[jb * 128 : jb * 128 + 128, cols].T
        return carry

    lax.fori_loop(0, 8, turn_filter, 0)
    load_weight[0].wait()
    for part, quarter in enumerate((partner, TP - 1 - partner)):
        fetch_out[part * 256 : part * 256 + 256, :] = weight[
            quarter_rows(mine), columns(quarter)
        ].astype(F32)
    pl.semaphore_wait(barrier, CTX + 1)

    edge = pltpu.make_async_remote_copy(
        src_ref=projected_hbm.at[:, 504:512, :],
        dst_ref=halo_in,
        send_sem=halo_send,
        recv_sem=halo_recv,
        device_id=(lax.rem(me + 1, CTX), tp),
        device_id_type=MESH,
    )
    edge.start()
    for half in range(2):
        part = pl.ds(2 * half, 2)
        send_slabs(
            filt_t.at[part], filt.at[part], rows_of, rows_of(me), me, tp, filt_send, filt_recv
        )
    fetch(0).start()
    fetch(1).start()
    load_projected.wait()
    load_tables = [
        pltpu.make_async_copy(source, target, load_sem.at[3 + i])
        for i, (source, target) in enumerate(
            (
                (first_hbm, first), (twist_hbm, twist), (second_hbm, second),
                (back_second_hbm, back_second), (back_first_hbm, back_first),
            )
        )
    ]
    for load in load_tables:
        load.start()
    for load in load_weight[1:]:
        load.start()
    edge.wait()
    halo[...] = jnp.where(me > 0, halo_in[...], 0.0)

    def gate(cb, carry):
        cols = pl.ds(pl.multiple_of(cb * 128, 128), 128)
        for jb in range(4):
            key = short_conv(projected, halo, short_filters, 1, jb, cols)
            value = short_conv(projected, halo, short_filters, 2, jb, cols)
            product = key * value
            gated[jb * 128 : jb * 128 + 128, cols] = product
            gated_t[jb, cols, :] = product.T
        return carry

    lax.fori_loop(0, 8, gate, 0)

    def send_group(group, carry):
        def slab(device):
            return pl.ds(pl.multiple_of(device * OWN + group * GROUP, GROUP), GROUP)

        send_slabs(
            gated_t, signal.at[group], slab, pl.ds(pl.multiple_of(me * GROUP, GROUP), GROUP),
            me, tp, signal_send, signal_recv.at[group],
        )
        return carry

    lax.fori_loop(0, GROUPS, send_group, 0)

    def query(cb, carry):
        cols = pl.ds(pl.multiple_of(cb * 128, 128), 128)
        for jb in range(4):
            shortened_q[jb * 128 : jb * 128 + 128, cols] = short_conv(
                projected, halo, short_filters, 0, jb, cols
            )
        return carry

    lax.fori_loop(0, 8, query, 0)

    load_weight[2].wait()
    for part, quarter in enumerate((partner, TP - 1 - partner)):
        rest = pl.ds(pl.multiple_of(theirs * 256 + 192, 64), 64)
        projected[2, part * 64 : part * 64 + 64, :] = weight[rest, columns(quarter)].astype(F32)
        fetch_rest(part).start()

    for load in load_tables:
        load.wait()
    cosine, sine = twist[0], twist[1]

    def forward(load_block):
        for i in range(GROUP):
            blocks = [load_block(i, jb) for jb in range(4)]
            high, low = split(
                jnp.concatenate(
                    [jnp.concatenate(blocks[:2], 1), jnp.concatenate(blocks[2:], 1)], 0
                )
            )
            turned = dot(first[...], jnp.concatenate([high, low, high], 0))
            real, imag = turned[:64], turned[64:]
            real_high, real_low = split(real * cosine + imag * sine)
            imag_high, imag_low = split(imag * cosine - real * sine)
            rows[i * 64 : i * 64 + 64, :] = jnp.concatenate(
                [real_high, imag_high, real_low, imag_low, real_high, imag_high], 1
            )
        return dot(rows[...], second[...])

    def group_rows(group):
        return pl.ds(pl.multiple_of(group * GROUP * 64, GROUP * 64), GROUP * 64)

    def filter_step(group, carry):
        spectrum[group_rows(group), :] = forward(
            lambda i, jb: filt[jb, pl.ds(group * GROUP + i, CTX, stride=OWN), :]
        )
        return carry

    wait_arrived(filt, filt_recv)
    lax.fori_loop(0, GROUPS, filter_step, 0)

    def signal_step(group, carry):
        left = forward(lambda i, jb: signal[group, jb, pl.ds(i, CTX, stride=GROUP), :])
        right = spectrum[group_rows(group), :]
        left_real, left_imag = left[:, :256], left[:, 256:]
        right_real, right_imag = right[:, :256], right[:, 256:]
        real_high, real_low = split(left_real * right_real - left_imag * right_imag)
        imag_high, imag_low = split(left_real * right_imag + left_imag * right_real)
        product = jnp.concatenate(
            [real_high, imag_high, real_low, imag_low, real_high, imag_high], 1
        )
        spectrum[group_rows(group), :] = dot(product, back_second[...])
        back(0, group)
        return carry

    def back(half, group):
        lanes = slice(128 * half, 128 * half + 128)
        imag_lanes = slice(256 + 128 * half, 384 + 128 * half)
        cosine, sine = twist[0, :, lanes], twist[1, :, lanes]
        for i in range(GROUP):
            channel = group * GROUP + i
            block = pl.ds(pl.multiple_of(channel * 64, 64), 64)
            real, imag = spectrum[block, lanes], spectrum[block, imag_lanes]
            real_high, real_low = split(real * cosine - imag * sine)
            imag_high, imag_low = split(imag * cosine + real * sine)
            result = dot(
                back_first[...],
                jnp.concatenate(
                    [real_high, imag_high, real_low, imag_low, real_high, imag_high], 0
                ),
            )
            conv[half, pl.ds(channel, CTX, stride=OWN), :] = result[:32]
            conv[half + 2, pl.ds(channel, CTX, stride=OWN), :] = result[32:]

    def back_step(group, carry):
        back(1, group)
        return carry

    def return_chunk(jb, first_row=0, count=OWN):
        chunk = pl.ds(jb, 1)

        def slab(device):
            return pl.ds(pl.multiple_of(device * OWN + first_row, GROUP), count)

        send_slabs(
            conv.at[chunk], conv_in.at[chunk], slab, slab(me),
            me, tp, conv_send.at[jb], conv_recv.at[jb],
        )

    wait_sent(filt_t, filt_send)
    def early_step(group, carry):
        wait_arrived(signal.at[group], signal_recv.at[group])
        return signal_step(group, carry)

    lax.fori_loop(0, GROUPS - 1, early_step, 0)
    return_chunk(0, 0, OWN - GROUP)
    wait_arrived(signal.at[GROUPS - 1], signal_recv.at[GROUPS - 1])
    for part in range(2):
        fetch(part).wait_recv()
    swap(3).start()
    signal_step(GROUPS - 1, 0)
    return_chunk(0, OWN - GROUP, GROUP)
    return_chunk(2)
    share(0)
    share(1)
    load_weight[1].wait()
    load_weight[3].wait()
    for part in range(2):
        fetch(part).wait_send()
        fetch_rest(part).wait_send()
        fetch_rest(part).wait_recv()
    swap(2).start()

    def gather(jb, half):
        tokens = pl.ds(64 * half, 64)
        return to_tp(
            gather_out(jb).at[tokens, :], gather_in.at[jb, tokens, :],
            partner, gather_send.at[jb, half], gather_recv.at[jb, half],
        )

    def send_sum(jb, half):
        tokens = pl.ds(64 * half, 64)
        return to_tp(
            sum_out(jb).at[tokens, :], sum_in.at[jb, tokens, :],
            mate, sum_send.at[jb, half], sum_recv.at[jb, half],
        )

    def gate_chunk(jb):
        wait_arrived(conv_in.at[pl.ds(jb, 1)], conv_recv.at[jb])
        tokens = slice(jb * 128, jb * 128 + 128)
        mixed = conv_in[jb].T + skip_gain[...] * gated[tokens, :]
        gated_out[jb] = (shortened_q[tokens, :] * mixed).astype(BF16)
        if jb:
            gather_out(jb)[...] = gated_out[jb].astype(F32)

    def start_gather(jb):
        for half in range(2):
            gather(jb, half).start()

    def gather_sent(jb):
        for half in range(2):
            gather(jb, half).wait_send()

    def push_sums(jb, half):
        tokens = slice(64 * half, 64 * half + 64)
        gather(jb, half).wait_recv()
        partner_out[tokens, :] = gather_in[jb, tokens, :].astype(BF16)
        sum_out(jb)[tokens, :] = dot(gated_out[jb, tokens, :], weight[:, columns(mate)]) + dot(
            partner_out[tokens, :], partner_weight[:, 1024:]
        )
        send_sum(jb, half).start()

    def keep_sums(jb):
        kept[jb * 128 : jb * 128 + 128, :] = dot(gated_out[jb], weight[:, columns(tp)]) + dot(
            partner_out[...], partner_weight[:, :1024]
        )
        store(jb).start()

    def store(jb):
        tokens = pl.ds(jb * 128, 128)
        return pltpu.make_async_copy(
            kept.at[tokens, :], kept_hbm.at[tokens, :], kept_sem.at[jb]
        )

    halves = (slice(0, 512), slice(512, 1024))

    def to_far(side):
        return to_tp(
            far.at[:, halves[1 - side]], far_in.at[:, halves[1 - side]],
            (mate, partner)[side], far_send.at[side], far_recv.at[side],
        )

    def to_near(side, part):
        half = halves[side] if part else halves[1 - side]
        return to_tp(
            near[side].at[:, half], near_in[side].at[:, half],
            (mate, partner)[side], near_send.at[side, part], near_recv.at[side, part],
        )

    def relay(side):
        to_far(1 - side).wait_recv()
        near[side][:, halves[side]] += far_in[:, halves[side]]
        to_near(side, 1).start()

    gate_chunk(0)
    for side in range(2):
        first_column = lax.rem(tp + 2, TP) * 1024 + 512 * (1 - side)
        far[:, halves[1 - side]] = dot(
            gated_out[0], weight[:, pl.ds(pl.multiple_of(first_column, 512), 512)]
        )
        to_far(side).start()
    near[0][...] = dot(gated_out[0], weight[:, columns(mate)])
    to_near(0, 0).start()
    lax.fori_loop(0, GROUPS, back_step, 0)
    return_chunk(1)
    return_chunk(3)
    gate_chunk(2)
    start_gather(2)
    relay(0)
    near[1][...] = dot(gated_out[0], weight[:, columns(partner)])
    kept[0:128, :] = dot(gated_out[0], weight[:, columns(tp)])
    store(0).start()
    swap(3).wait_recv()
    round_quarters(0)
    for part in range(2):
        wait_arrived(shared(theirs, part), share_recv.at[part])
        swap(part).start()
    for part in range(3):
        swap(part).wait_recv()
    round_quarters(1)
    to_near(1, 0).start()
    gate_chunk(1)
    gather_sent(2)
    start_gather(1)
    push_sums(2, 0)
    push_sums(2, 1)
    keep_sums(2)
    gate_chunk(3)
    push_sums(1, 0)
    gather_sent(1)
    start_gather(3)
    push_sums(1, 1)
    keep_sums(1)
    push_sums(3, 0)
    relay(1)
    push_sums(3, 1)
    keep_sums(3)
    gather_sent(3)
    for side in range(2):
        to_far(side).wait_send()
        for part in range(2):
            to_near(side, part).wait()
    for jb in range(4):
        store(jb).wait()
        if jb:
            for half in range(2):
                send_sum(jb, half).wait()
    wait_sent(gated_t, signal_send)
    for part in range(2):
        wait_arrived(shared(mine, part), share_send.at[part])
        swap(part).wait_send()
    swap(2).wait_send()
    swap(3).wait_send()
    for jb in range(4):
        wait_sent(conv.at[pl.ds(jb, 1)], conv_send.at[jb])


def add_kernel(kept, landed, landed_chunk, total, left, right, first_chunk, load_sem, store_sem):
    chunks = [pl.ds(128 * jb, 128) for jb in range(4)]
    loads = [pltpu.make_async_copy(landed_chunk, first_chunk, load_sem.at[8])]
    for jb, chunk in enumerate(chunks):
        loads.append(pltpu.make_async_copy(kept.at[chunk, :], left.at[chunk, :], load_sem.at[jb]))
        loads.append(
            pltpu.make_async_copy(landed.at[chunk, :], right.at[chunk, :], load_sem.at[4 + jb])
        )
    for load in loads:
        load.start()
    loads[0].wait()
    stores = []
    for jb, chunk in enumerate(chunks):
        loads[1 + 2 * jb].wait()
        loads[2 + 2 * jb].wait()
        value = left[chunk, :] + right[chunk, :]
        left[chunk, :] = value + first_chunk[...] if jb == 0 else value
        stores.append(
            pltpu.make_async_copy(left.at[chunk, :], total.at[chunk, :], store_sem.at[jb])
        )
        stores[jb].start()
    for store in stores:
        store.wait()


VMEM = pl.BlockSpec(memory_space=pltpu.VMEM)
HBM = pl.BlockSpec(memory_space=pltpu.HBM)
DMA = pltpu.SemaphoreType.DMA


def per_device(projected, short_filters, long_filter, skip_gain, out_weight):
    kept, landed, landed_chunk = pl.pallas_call(
        mixer_kernel,
        out_shape=(
            jax.ShapeDtypeStruct((512, 1024), F32),
            jax.ShapeDtypeStruct((4, 128, 1024), F32),
            jax.ShapeDtypeStruct((128, 1024), F32),
        ),
        in_specs=[HBM, VMEM, HBM, VMEM, HBM] + [HBM] * 5,
        out_specs=(HBM, HBM, HBM),
        scratch_shapes=[
            pltpu.VMEM((512, 1024), F32),
            pltpu.VMEM((3, 512, 1024), F32),
            pltpu.VMEM((512, 1024), F32),
            pltpu.VMEM((1024, 4096), BF16),
            pltpu.VMEM((128, 192), BF16),
            pltpu.VMEM((2, 64, 256), F32),
            pltpu.VMEM((1536, 512), BF16),
            pltpu.VMEM((1536, 512), BF16),
            pltpu.VMEM((64, 384), BF16),
            pltpu.VMEM((3, 8, 1024), F32),
            pltpu.VMEM((3, 8, 1024), F32),
            pltpu.VMEM((4, 1024, 128), F32),
            pltpu.VMEM((4, 1024, 128), F32),
            pltpu.VMEM((4, 1024, 128), F32),
            pltpu.VMEM((GROUPS, 4, CTX * GROUP, 128), F32),
            pltpu.VMEM((512, 1024), F32),
            pltpu.VMEM((GROUP * 64, 1536), BF16),
            pltpu.VMEM((OWN * 64, 512), F32),
            pltpu.VMEM((4, 1024, 128), F32),
            pltpu.VMEM((4, 128, 1024), BF16),
            pltpu.VMEM((128, 1024), BF16),
            pltpu.VMEM((1024, 2048), F32),
            pltpu.VMEM((1024, 2048), BF16),
            pltpu.VMEM((4, 128, 1024), F32),
            DMA((12,)),
            DMA,
            DMA,
            DMA,
            DMA,
            DMA,
            DMA((GROUPS,)),
            DMA((4,)),
            DMA((4,)),
            DMA((4,)),
            DMA((4,)),
            DMA((2,)),
            DMA((2,)),
            DMA((4,)),
            DMA((4,)),
            DMA((4, 2)),
            DMA((4, 2)),
            DMA((4, 2)),
            DMA((4, 2)),
            DMA((2,)),
            DMA((2,)),
            DMA((2, 2)),
            DMA((2, 2)),
            DMA((4,)),
        ],
        compiler_params=pltpu.CompilerParams(
            collective_id=0, has_side_effects=True, vmem_limit_bytes=60 * 2**20
        ),
        name="mixer",
    )(
        projected, short_filters, long_filter, skip_gain[None], out_weight,
        *[jnp.asarray(table) for table in tables()],
    )
    return pl.pallas_call(
        add_kernel,
        out_shape=jax.ShapeDtypeStruct((512, 1024), F32),
        in_specs=[HBM] * 3,
        out_specs=HBM,
        scratch_shapes=[
            pltpu.VMEM((512, 1024), F32),
            pltpu.VMEM((512, 1024), F32),
            pltpu.VMEM((128, 1024), F32),
            DMA((9,)),
            DMA((4,)),
        ],
        compiler_params=pltpu.CompilerParams(vmem_limit_bytes=60 * 2**20),
        name="add",
    )(kept, landed.reshape(512, 1024), landed_chunk)


def solution(mesh):
    return jax.shard_map(
        per_device,
        mesh=mesh,
        in_specs=(
            P(None, "ctx", "tp"),
            P(None, None, "tp"),
            P("ctx", "tp"),
            P("tp"),
            P("tp", None),
        ),
        out_specs=P("ctx", "tp"),
        check_vma=False,
    )
```
